128 devices in a mesh: score: 8 (over z, core), mp: 16 (over y, x).
Axes of the slice: x: 4, y: 4, z: 4, core: 2. Of those that a mesh axis runs over, the one named last changes fastest.
Arguments:
- tokens: bfloat16 [48, 256, 3584], P('score', 'mp'), may hold values from -150 to 150
- gain: float32 [3584], replicated, may hold values from 0.1 to 1.9
- w_query: bfloat16 [3584, 2048], P(None, 'mp'), may hold values from -0.09375 to 0.09375
- b_query: float32 [2048], P('mp'), may hold values from -3 to 3
- w_key: bfloat16 [3584, 512], replicated, may hold values from -0.1875 to 0.1875
- b_key: float32 [512], replicated, may hold values from -3 to 3
- w_value: bfloat16 [3584, 512], replicated, may hold values from -0.75 to 0.75
- b_value: float32 [512], replicated, may hold values from -12 to 12
- rubric_cache: bfloat16 [8, 4, 2048, 256], P('score', None, 'mp'), may hold values from -420 to 420
- dest_of: int32 [48], replicated, may hold values from 0 to 7, as said below
- lengths: int32 [48], replicated, may hold values from 64 to 256
Outputs:
- rubric_attention: bfloat16 [8, 8, 256, 2048], P('score', None, None, 'mp')
The draws below stay inside these ranges and needn't reach their ends.
Inputs may be any that keep to these rules, and one draw needn't show every extreme that they name: `dest_of`: the 6 responses of one rollout group go to 6 different scorer groups. In every draw one scorer group receives a response from every rollout group, and each of those has 256 tokens.
All inputs are finite; a program needn't handle non-finite values.
Results may differ from the reference program's by a relative error of at most 0.013.
The reference program's roundings to bfloat16 on the way count: a program that leaves them out, or rounds other values in their place, can miss the bound.
Values may be sent and summed in bfloat16 or wider, within the bound.
No kernel may reach another device: no remote copies, remote signals or barrier semaphores. Data moves between devices by JAX's collectives and lax.ppermute only.
A program may use at most 128 MiB of HBM per device.

```python
import math
import jax
import jax.numpy as jnp
from jax import lax

D = 3584
HEADS = 16
KV_HEADS = 4
HD = 128
LEN_MAX = 256
LEN_MIN = 64
PROMPT = 2048
RESP_GRP = 6
N_SCORE = 8


def packing_table(key):
    key_favored, key_pick, key_order, key_length = jax.random.split(key, 4)
    favored = jax.random.randint(key_favored, (), 0, N_SCORE)
    columns = jnp.arange(N_SCORE, dtype=jnp.int32)
    ranking = jax.random.randint(key_pick, (N_SCORE, N_SCORE), 0, 2 ** 20) * N_SCORE + columns[None, :]
    ranking = ranking + jnp.where(columns[None, :] == favored, 2 ** 26, 0)
    ignored, chosen = lax.top_k(ranking, RESP_GRP)
    shuffle = jax.random.randint(key_order, (N_SCORE, RESP_GRP), 0, 2 ** 20) * RESP_GRP + jnp.arange(RESP_GRP, dtype=jnp.int32)[None, :]
    ordering = jnp.argsort(shuffle, axis=1)
    targets = jnp.take_along_axis(chosen, ordering, axis=1)
    sizes_drawn = jax.random.randint(key_length, (N_SCORE, RESP_GRP), LEN_MIN, LEN_MAX + 1)
    sizes_drawn = jnp.where(targets == favored, LEN_MAX, sizes_drawn)
    return (targets.reshape(-1).astype(jnp.int32), sizes_drawn.reshape(-1).astype(jnp.int32))


def draw_dest_of(key, part):
    return packing_table(key)[0]


def draw_lengths(key, part):
    return packing_table(key)[1]


def draw_tokens(key, part):
    key = jax.random.fold_in(key, 5)
    key_base, key_rows, key_cols = jax.random.split(key, 3)
    full_shape = (N_SCORE * RESP_GRP, LEN_MAX, D)
    row_scale = jnp.exp(jax.random.uniform(key_rows, (N_SCORE * RESP_GRP, LEN_MAX, 1), jnp.float32, 0.0, math.log(10.0)))
    col_scale = jnp.exp(jax.random.uniform(key_cols, (1, 1, D), jnp.float32, math.log(0.3), math.log(3.0)))
    base = jnp.clip(jax.random.normal(key_base, full_shape, jnp.float32), -5.0, 5.0)
    return (base * row_scale * col_scale).astype(jnp.bfloat16)


def draw_rubric_cache(key, part):
    key = jax.random.fold_in(key, 11)
    key_keys, key_values = jax.random.split(key, 2)
    half_shape = (N_SCORE, KV_HEADS, PROMPT, HD)
    keys_part = 1.4 * jnp.clip(jax.random.normal(key_keys, half_shape, jnp.float32), -6.0, 6.0)
    values_part = 8.0 * jnp.clip(jax.random.normal(key_values, half_shape, jnp.float32), -6.0, 6.0)
    return jnp.concatenate([keys_part, values_part], axis=-1).astype(jnp.bfloat16)


def block_scale(stream_key, dims, pieces, low, top_value):
    level = 1.0
    for dim, shards_of in pieces:
        steps = jax.random.uniform(jax.random.fold_in(jax.random.fold_in(stream_key, 6), dim), (shards_of,), jnp.float32, low / len(pieces), top_value / len(pieces))
        level = level * jnp.repeat(jnp.exp(steps), dims[dim] // shards_of).reshape((-1,) + (1,) * (len(dims) - 1 - dim))
    return level


def centred(key, dims, spread, most, cuts=(), kind=jnp.bfloat16):
    factor_of = block_scale(key, dims, cuts, -0.22, 0.18) if cuts else 1.0
    values = jax.random.normal(key, dims, jnp.float32) * spread * factor_of
    return jnp.minimum(jnp.maximum(values, -most), most).astype(kind)


def setup_inputs(seed: int = 0) -> dict:
    key_of = jax.random.split(jax.random.key(seed), 12)
    return {
        "tokens": draw_tokens(jax.random.fold_in(key_of[11], 71), 0),
        "gain": jnp.clip(1.0 + 0.18 * jax.random.normal(key_of[1], (D,), jnp.float32), 0.1, 1.9),
        "w_query": centred(key_of[2], (D, HEADS * HD), D ** -0.5, 0.09375, ((1, 16),)),
        "b_query": centred(key_of[3], (HEADS * HD,), 0.5, 3.0, ((0, 16),), jnp.float32),
        "w_key": centred(key_of[4], (D, KV_HEADS * HD), (D // 4) ** -0.5, 0.1875),
        "b_key": centred(key_of[5], (KV_HEADS * HD,), 0.5, 3.0, (), jnp.float32),
        "w_value": centred(key_of[6], (D, KV_HEADS * HD), (D // 64) ** -0.5, 0.75),
        "b_value": centred(key_of[7], (KV_HEADS * HD,), 2.0, 12.0, (), jnp.float32),
        "rubric_cache": draw_rubric_cache(jax.random.fold_in(key_of[11], 71), 0),
        "dest_of": draw_dest_of(jax.random.fold_in(key_of[11], 71), 0),
        "lengths": draw_lengths(jax.random.fold_in(key_of[11], 71), 0),
    }


THETA = 1000000.0
EPSILON = 1e-06

def rotate(vectors, positions):
    half_width = vectors.shape[-1] // 2
    frequency = jnp.exp(jnp.arange(half_width, dtype=jnp.float32) * (-2.0 * math.log(THETA) / vectors.shape[-1]))
    angles = positions.astype(jnp.float32)[:, None] * frequency[None, :]
    cosine = jnp.cos(angles)[:, None, :]
    sine = jnp.sin(angles)[:, None, :]
    first = vectors[..., :half_width]
    second = vectors[..., half_width:]
    return jnp.concatenate([first * cosine - second * sine, second * cosine + first * sine], axis=-1)

def attend(queries, keys_self, values_self, slot_lengths, rubric_keys, rubric_values):
    head_width = queries.shape[-1]
    slot_span = queries.shape[1]
    score_scale = 1.0 / math.sqrt(head_width)
    rubric_scores = jnp.einsum('blhe,pe->blhp', queries.astype(jnp.float32), rubric_keys.astype(jnp.float32)) * score_scale
    self_scores = jnp.einsum('blhe,bke->blhk', queries.astype(jnp.float32), keys_self.astype(jnp.float32)) * score_scale
    positions = jnp.arange(slot_span)
    allowed = (positions[None, :] <= positions[:, None])[None, :, None, :] & (positions[None, :] < slot_lengths[:, None])[:, None, None, :]
    self_scores = jnp.where(allowed, self_scores, -jnp.inf)
    row_max = jnp.maximum(lax.optimization_barrier(jnp.max(rubric_scores, axis=-1)), lax.optimization_barrier(jnp.max(self_scores, axis=-1)))
    rubric_exp = jnp.exp(rubric_scores - row_max[..., None])
    self_exp = jnp.exp(self_scores - row_max[..., None])
    denominator = lax.optimization_barrier(jnp.sum(rubric_exp, axis=-1)) + lax.optimization_barrier(jnp.sum(self_exp, axis=-1))
    rubric_weights = (rubric_exp / denominator[..., None]).astype(jnp.bfloat16)
    self_weights = (self_exp / denominator[..., None]).astype(jnp.bfloat16)
    mixed = jnp.einsum('blhp,pe->blhe', rubric_weights.astype(jnp.float32), rubric_values.astype(jnp.float32))
    mixed = mixed + jnp.einsum('blhk,bke->blhe', self_weights.astype(jnp.float32), values_self.astype(jnp.float32))
    live_rows = positions[None, :] < slot_lengths[:, None]
    mixed = jnp.where(live_rows[:, :, None, None], mixed, jnp.zeros_like(mixed))
    return mixed.reshape(queries.shape[0], slot_span, -1).astype(jnp.bfloat16)

def reference(tokens, gain, w_query, b_query, w_key, b_key, w_value, b_value, rubric_cache, dest_of, lengths):
    per_group = tokens.reshape(N_SCORE, RESP_GRP, LEN_MAX, D)
    targets = dest_of.reshape(N_SCORE, RESP_GRP)
    lengths_all = lengths.reshape(N_SCORE, RESP_GRP)
    cache = lax.dynamic_index_in_dim(rubric_cache, dest_of[0], 0, keepdims=False)
    group_size = HEADS // KV_HEADS
    positions = PROMPT + jnp.arange(LEN_MAX, dtype=jnp.int32)

    def score_group(target):
        arrived_hit = targets == target
        chosen = lax.optimization_barrier(jnp.sum(jnp.where(arrived_hit, jnp.arange(RESP_GRP, dtype=jnp.int32)[None, :], 0), axis=1)).astype(jnp.int32)
        present = jnp.any(arrived_hit, axis=1)
        slot_lengths = lax.optimization_barrier(jnp.sum(jnp.where(arrived_hit, lengths_all, 0), axis=1)).astype(jnp.int32)
        slots = per_group[jnp.arange(N_SCORE, dtype=jnp.int32), chosen]
        slots = jnp.where(present[:, None, None], slots, jnp.zeros_like(slots))
        wide = slots.reshape(N_SCORE * LEN_MAX, D).astype(jnp.float32)
        normed = (wide * lax.rsqrt(lax.optimization_barrier(jnp.mean(wide * wide, axis=-1, keepdims=True)) + EPSILON) * gain).astype(jnp.bfloat16)
        query_raw = jnp.dot(normed, w_query, preferred_element_type=jnp.float32) + b_query
        queries = rotate(query_raw.reshape(N_SCORE, LEN_MAX, HEADS, HD), positions).astype(jnp.bfloat16)
        key_raw = jnp.dot(normed, w_key, preferred_element_type=jnp.float32) + b_key
        keys_self = rotate(key_raw.reshape(N_SCORE, LEN_MAX, KV_HEADS, HD), positions).astype(jnp.bfloat16)
        value_raw = jnp.dot(normed, w_value, preferred_element_type=jnp.float32) + b_value
        values_self = value_raw.astype(jnp.bfloat16).reshape(N_SCORE, LEN_MAX, KV_HEADS, HD)
        grouped = queries.reshape(N_SCORE, LEN_MAX, KV_HEADS, group_size, HD).transpose(2, 0, 1, 3, 4)

        def per_head(members):
            return attend(members[0], members[1], members[2], slot_lengths, members[3][:, :HD], members[3][:, HD:])
        outputs = lax.map(per_head, (grouped, keys_self.transpose(2, 0, 1, 3), values_self.transpose(2, 0, 1, 3), cache))
        return outputs.transpose(1, 2, 0, 3).reshape(N_SCORE, LEN_MAX, HEADS * HD)
    return lax.map(score_group, jnp.arange(N_SCORE, dtype=jnp.int32))
```

```python
import math

import jax
import jax.numpy as jnp
from jax import lax
from jax.experimental import pallas as pl
from jax.experimental.pallas import tpu as pltpu
from jax.sharding import PartitionSpec as P

D = 3584
KV_HEADS = 4
HD = 128
LEN_MAX = 256
PROMPT = 2048
RESP = 6
GROUPS = 8
HALF_D = D // 2
BIAS_ROWS = 16
CHUNK = RESP * 16
THETA = 1000000.0
EPSILON = 1e-06
SCALE = 1.0 / math.sqrt(HD)
LOG2E = math.log2(math.e)
AXES = ("score", "mp")
VMEM_LIMIT = 48 * 1024 * 1024


def device_number(x, y, z, c):
    return (z * 2 + c) * 16 + y * 4 + x


def shift(v, dx=0, dy=0, dz=0, flip=0):
    pairs = []
    for x in range(4):
        for y in range(4):
            for z in range(4):
                for c in range(2):
                    target = device_number((x + dx) % 4, (y + dy) % 4, (z + dz) % 4, c ^ flip)
                    pairs.append((device_number(x, y, z, c), target))
    return lax.ppermute(v, AXES, pairs)


X_GROUPS = [[y * 4 + x for x in range(4)] for y in range(4)]
SCORE_X_GROUPS = [[s * 16 + y * 4 + x for s in range(8) for x in range(4)] for y in range(4)]


def params():
    return pltpu.CompilerParams(vmem_limit_bytes=VMEM_LIMIT)


VMEM_SPEC = pl.BlockSpec(memory_space=pltpu.VMEM)
SMEM_SPEC = pl.BlockSpec(memory_space=pltpu.SMEM)


def norm_kernel(tokens_ref, gain_ref, out_ref):
    wide = tokens_ref[...].astype(jnp.float32)
    mean = jnp.mean(wide * wide, axis=-1, keepdims=True)
    out_ref[...] = (wide * lax.rsqrt(mean + EPSILON) * gain_ref[...]).astype(jnp.bfloat16)


def norm_rows(tokens, gain):
    return pl.pallas_call(
        norm_kernel,
        out_shape=jax.ShapeDtypeStruct((CHUNK, D), jnp.bfloat16),
        in_specs=[VMEM_SPEC, VMEM_SPEC],
        out_specs=VMEM_SPEC,
        compiler_params=params(),
        name="norm_rows",
    )(tokens, gain)


def rope(v, cos, sin):
    return v * cos + pltpu.roll(v, 64, axis=1) * sin


def chunk_y(y, j):
    return lax.rem(y + (0, 3, 1, 2)[j], 4)


def fill_rows(rows, own, before, after, far_a, far_b):
    rows[pl.ds(0, CHUNK), :] = own[...]
    rows[pl.ds(CHUNK, CHUNK), :] = before[...]
    rows[pl.ds(2 * CHUNK, CHUNK), :] = after[...]
    rows[pl.ds(3 * CHUNK, CHUNK // 2), :] = far_a[...]
    rows[pl.ds(3 * CHUNK + CHUNK // 2, CHUNK // 2), :] = far_b[...]


def kv_kernel(meta, own, before, after, far_a, far_b, wk, wv, bk, bv, cos_ref, sin_ref, out, rows):
    y = meta[0]
    fill_rows(rows, own, before, after, far_a, far_b)
    w = jnp.concatenate([wk[...], wv[...]], axis=1)
    both = jnp.dot(rows[...], w, preferred_element_type=jnp.float32)
    key_bias = bk[...]
    value_bias = bv[...]
    for j in range(4):
        base = pl.multiple_of(chunk_y(y, j) * 16, 16)
        cos = cos_ref[pl.ds(base, 16), :]
        sin = sin_ref[pl.ds(base, 16), :]
        for i in range(RESP):
            part = both[j * CHUNK + i * 16 : j * CHUNK + i * 16 + 16, :]
            key = rope(part[:, :HD] + key_bias, cos, sin).astype(jnp.bfloat16)
            value = (part[:, HD:] + value_bias).astype(jnp.bfloat16)
            out[i, pl.ds(base, 16), 0:HD] = key
            out[i, pl.ds(base, 16), HD : 2 * HD] = value


def own_keys_values(meta, chunks, w_key, w_value, b_key, b_value, cos, sin):
    whole = lambda shape: pl.BlockSpec(shape, lambda s, m: (0,) * len(shape))
    column = lambda rows: pl.BlockSpec((rows, HD), lambda s, m: (0, m[0]))
    return pl.pallas_call(
        kv_kernel,
        out_shape=jax.ShapeDtypeStruct((RESP, 64, 2 * HD), jnp.bfloat16),
        grid_spec=pltpu.PrefetchScalarGridSpec(
            num_scalar_prefetch=1,
            grid=(1,),
            in_specs=[whole(c.shape) for c in chunks]
            + [column(D), column(D), column(1), column(1), whole((64, HD)), whole((64, HD))],
            out_specs=whole((RESP, 64, 2 * HD)),
            scratch_shapes=[pltpu.VMEM((4 * CHUNK, D), jnp.bfloat16)],
        ),
        compiler_params=params(),
        name="keys_values",
    )(meta, *chunks, w_key, w_value, b_key, b_value, cos, sin)


def query_kernel(
    meta, own, before, after, far_a, far_b, w_mine, w_other, cos_ref, sin_ref, c_mine, c_other,
    q_out, acc_out, stat_out, rows,
):
    y = meta[0]
    c = meta[1]
    fill_rows(rows, own, before, after, far_a, far_b)
    mine_at = pl.multiple_of(c * HALF_D, 128)
    other_at = pl.multiple_of((1 - c) * HALF_D, 128)
    for pair in range(2):
        lo, hi = 2 * pair, 2 * pair + 1
        wm = jnp.concatenate([w_mine[lo, :HALF_D, :], w_mine[hi, :HALF_D, :]], axis=1)
        wo = jnp.concatenate([w_other[lo, :HALF_D, :], w_other[hi, :HALF_D, :]], axis=1)
        both = jnp.dot(rows[:, pl.ds(mine_at, HALF_D)], wm, preferred_element_type=jnp.float32)
        both = both + jnp.dot(rows[:, pl.ds(other_at, HALF_D)], wo, preferred_element_type=jnp.float32)
        for h in (lo, hi):
            tail = w_mine[h, HALF_D : HALF_D + BIAS_ROWS, :].astype(jnp.float32)
            bias = tail[0:1, :] + tail[1:2, :] + tail[2:3, :]
            raw = both[:, (h - lo) * HD : (h - lo + 1) * HD] + bias
            for j in range(4):
                base = pl.multiple_of(chunk_y(y, j) * 16, 16)
                cos = cos_ref[pl.ds(base, 16), :]
                sin = sin_ref[pl.ds(base, 16), :]
                for i in range(RESP):
                    part = raw[j * CHUNK + i * 16 : j * CHUNK + i * 16 + 16, :]
                    q_out[i, h, pl.ds(base, 16), :] = rope(part, cos, sin).astype(jnp.bfloat16)

    def step(i, carry):
        q = q_out[i].reshape(4 * 64, HD)
        keys = jnp.concatenate([c_mine[:, :HD], c_other[:, :HD]], axis=0)
        scores = lax.dot_general(q, keys, (((1,), (1,)), ((), ())), preferred_element_type=jnp.float32)
        top = jnp.max(scores, axis=-1, keepdims=True)
        weights = jnp.exp2(scores * (SCALE * LOG2E) - top * (SCALE * LOG2E))
        total = jnp.sum(weights, axis=-1, keepdims=True)
        values = jnp.concatenate([c_mine[:, HD:], c_other[:, HD:]], axis=0)
        acc_out[i] = jnp.dot(weights.astype(jnp.bfloat16), values, preferred_element_type=jnp.float32)
        lane = lax.broadcasted_iota(jnp.int32, (4 * 64, HD), 1)
        stat_out[i] = jnp.where(lane < 64, top, total)
        return carry

    lax.fori_loop(0, RESP, step, 0)


def rubric_part(meta, chunks, w_mine, w_other, cos, sin, c_mine, c_other):
    return pl.pallas_call(
        query_kernel,
        out_shape=(
            jax.ShapeDtypeStruct((RESP, 4, 64, HD), jnp.bfloat16),
            jax.ShapeDtypeStruct((RESP, 256, HD), jnp.float32),
            jax.ShapeDtypeStruct((RESP, 256, HD), jnp.float32),
        ),
        in_specs=[SMEM_SPEC] + [VMEM_SPEC] * 11,
        out_specs=(VMEM_SPEC, VMEM_SPEC, VMEM_SPEC),
        scratch_shapes=[pltpu.VMEM((4 * CHUNK, D), jnp.bfloat16)],
        compiler_params=params(),
        cost_estimate=pl.CostEstimate(
            flops=3_000_000_000, bytes_accessed=12_000_000, transcendentals=3_200_000
        ),
        name="rubric_part",
    )(meta, *chunks, w_mine, w_other, cos, sin, c_mine, c_other)


def self_kernel(meta, dest, lengths, q_ref, acc_ref, stat_ref, kv0, kv1, kv2, kv3, out):
    x = meta[2]
    g = meta[3]
    out[...] = jnp.zeros_like(out)
    row = lax.broadcasted_iota(jnp.int32, (256, 256), 0)
    col = lax.broadcasted_iota(jnp.int32, (256, 256), 1)
    slot_row = lax.rem(row, 64)
    row_pos = (slot_row // 16) * 64 + x * 16 + lax.rem(slot_row, 16)
    slot_col = lax.rem(col, 64)
    which = col // 64
    offset = jnp.where(which == 0, 0, jnp.where(which == 1, 3, jnp.where(which == 2, 1, 2)))
    col_x = lax.rem(x + offset, 4)
    col_pos = (slot_col // 16) * 64 + col_x * 16 + lax.rem(slot_col, 16)
    causal = col_pos <= row_pos
    one_pos = row_pos[:, 0:HD]
    for i in range(RESP):
        length = lengths[g * RESP + i]
        q = q_ref[i].reshape(256, HD)
        keys = jnp.concatenate([kv0[i, :, :HD], kv1[i, :, :HD], kv2[i, :, :HD], kv3[i, :, :HD]], axis=0)
        values = jnp.concatenate([kv0[i, :, HD:], kv1[i, :, HD:], kv2[i, :, HD:], kv3[i, :, HD:]], axis=0)
        scores = lax.dot_general(q, keys, (((1,), (1,)), ((), ())), preferred_element_type=jnp.float32)
        scores = jnp.where(causal & (col_pos < length), scores, -jnp.inf)
        far_top = stat_ref[i, :, 0:1]
        far_total = stat_ref[i, :, 64:65]
        top = jnp.maximum(jnp.max(scores, axis=-1, keepdims=True), far_top)
        weights = jnp.exp2((scores - top) * (SCALE * LOG2E))
        factor = jnp.exp2((far_top - top) * (SCALE * LOG2E))
        total = jnp.sum(weights, axis=-1, keepdims=True) + far_total * factor
        near = jnp.dot(weights.astype(jnp.bfloat16), values, preferred_element_type=jnp.float32)
        mixed = (acc_ref[i] * factor + near) / total
        mixed = jnp.where(one_pos < length, mixed, 0.0).astype(jnp.bfloat16)
        out[dest[g * RESP + i]] = mixed.reshape(4, 64, HD)


def self_part(meta, dest, lengths, q, acc, stat, parts):
    return pl.pallas_call(
        self_kernel,
        out_shape=jax.ShapeDtypeStruct((GROUPS, 4, 64, HD), jnp.bfloat16),
        in_specs=[SMEM_SPEC] * 3 + [VMEM_SPEC] * 7,
        out_specs=VMEM_SPEC,
        compiler_params=params(),
        name="self_part",
    )(meta, dest, lengths, q, acc, stat, *parts)


def on_device(
    tokens, gain, w_query, b_query, w_key, b_key, w_value, b_value, rubric_cache, dest_of, lengths
):
    g = lax.axis_index("score")
    m = lax.axis_index("mp")
    z, c = g // 2, g % 2
    y, x = m // 4, m % 4
    meta = jnp.stack([y, c, x, g]).astype(jnp.int32)

    normed = norm_rows(tokens.reshape(CHUNK, D), gain.reshape(1, D))
    before = shift(normed, dy=1)
    after = shift(normed, dy=-1)
    far_a = shift(before[: CHUNK // 2], dy=1)
    far_b = shift(after[CHUNK // 2 :], dy=-1)
    chunks = (normed, before, after, far_a, far_b)

    first = lax.reduce_precision(b_query, 8, 7)
    second = lax.reduce_precision(b_query - first, 8, 7)
    third = b_query - first - second
    tail = jnp.stack([first, second, third]).astype(jnp.bfloat16)
    tail = jnp.pad(tail, ((0, BIAS_ROWS - 3), (0, 0)))
    half = jnp.concatenate([lax.dynamic_slice_in_dim(w_query, c * HALF_D, HALF_D, 0), tail], axis=0)
    w_mine = lax.all_gather(half, "mp", axis=0, axis_index_groups=X_GROUPS)
    w_other = shift(w_mine, flip=1)

    owner = dest_of[0]
    cache = rubric_cache[0]
    swapped = shift(cache, flip=1)
    cache = jnp.where(owner % 2 == c, cache, swapped)
    piece = lax.dynamic_slice_in_dim(cache, c * 64, 64, 1)
    z_before = shift(piece, dz=1)
    z_after = shift(piece, dz=-1)
    z_far = shift(piece, dz=2)
    turn = (owner // 2 - z) % 4
    piece = jnp.where(
        turn == 0, piece, jnp.where(turn == 3, z_before, jnp.where(turn == 1, z_after, z_far))
    )
    spread = jnp.broadcast_to(piece[:, None], (4, 4, 64, 2 * HD)).reshape(16, 64, 2 * HD)
    c_mine = lax.all_to_all(spread, "mp", 0, 0, tiled=True).reshape(1024, 2 * HD)
    c_other = shift(c_mine, flip=1)

    frequency = jnp.exp(jnp.arange(64, dtype=jnp.float32) * (-2.0 * math.log(THETA) / HD))
    slot = jnp.arange(64, dtype=jnp.int32)
    positions = PROMPT + (slot // 16) * 64 + x * 16 + slot % 16
    angles = positions.astype(jnp.float32)[:, None] * frequency[None, :]
    cos = jnp.cos(angles)
    sin = jnp.sin(angles)
    cos = jnp.concatenate([cos, cos], axis=1)
    sin = jnp.concatenate([-sin, sin], axis=1)

    kv = own_keys_values(
        meta, chunks, w_key, w_value, b_key.reshape(1, -1), b_value.reshape(1, -1), cos, sin
    )
    parts = (kv, shift(kv, dx=1), shift(kv, dx=-1), shift(kv, dx=2))
    q, acc, stat = rubric_part(meta, chunks, w_mine, w_other, cos, sin, c_mine, c_other)
    ready = self_part(meta, dest_of, lengths, q, acc, stat, parts)
    arrived = lax.all_to_all(
        ready.reshape(32, 64, HD), AXES, 0, 0, tiled=True, axis_index_groups=SCORE_X_GROUPS
    )
    result = arrived.reshape(GROUPS, 4, 4, 16, HD).transpose(0, 2, 1, 3, 4)
    return result.reshape(1, GROUPS, LEN_MAX, HD)


def solution(mesh):
    in_specs = (
        P("score", "mp", None),
        P(),
        P(None, "mp"),
        P("mp"),
        P(),
        P(),
        P(),
        P(),
        P("score", None, "mp", None),
        P(),
        P(),
    )
    out_specs = P("score", None, None, "mp")
    return jax.shard_map(
        on_device, mesh=mesh, in_specs=in_specs, out_specs=out_specs, check_vma=False
    )
```

```python
import math

import jax
import jax.numpy as jnp
from jax import lax
from jax.experimental import pallas as pl
from jax.experimental.pallas import tpu as pltpu
from jax.sharding import PartitionSpec as P

D = 3584
KV_HEADS = 4
HD = 128
LEN_MAX = 256
PROMPT = 2048
RESP = 6
GROUPS = 8
HALF_D = D // 2
BIAS_ROWS = 16
CHUNK = RESP * 16
THETA = 1000000.0
EPSILON = 1e-06
SCALE = 1.0 / math.sqrt(HD)
LOG2E = math.log2(math.e)
AXES = ("score", "mp")
VMEM_LIMIT = 48 * 1024 * 1024


def device_number(x, y, z, c):
    return (z * 2 + c) * 16 + y * 4 + x


def shift(v, dx=0, dy=0, dz=0, flip=0):
    pairs = []
    for x in range(4):
        for y in range(4):
            for z in range(4):
                for c in range(2):
                    target = device_number((x + dx) % 4, (y + dy) % 4, (z + dz) % 4, c ^ flip)
                    pairs.append((device_number(x, y, z, c), target))
    return lax.ppermute(v, AXES, pairs)


X_GROUPS = [[y * 4 + x for x in range(4)] for y in range(4)]
SCORE_X_GROUPS = [[s * 16 + y * 4 + x for s in range(8) for x in range(4)] for y in range(4)]


def params():
    return pltpu.CompilerParams(vmem_limit_bytes=VMEM_LIMIT)


VMEM_SPEC = pl.BlockSpec(memory_space=pltpu.VMEM)
SMEM_SPEC = pl.BlockSpec(memory_space=pltpu.SMEM)


def norm_kernel(tokens_ref, gain_ref, out_ref):
    wide = tokens_ref[...].astype(jnp.float32)
    mean = jnp.mean(wide * wide, axis=-1, keepdims=True)
    out_ref[...] = (wide * lax.rsqrt(mean + EPSILON) * gain_ref[...]).astype(jnp.bfloat16)


def norm_rows(tokens, gain):
    return pl.pallas_call(
        norm_kernel,
        out_shape=jax.ShapeDtypeStruct((CHUNK, D), jnp.bfloat16),
        in_specs=[VMEM_SPEC, VMEM_SPEC],
        out_specs=VMEM_SPEC,
        compiler_params=params(),
        name="norm_rows",
    )(tokens, gain)


def rope(v, cos, sin):
    return v * cos + pltpu.roll(v, 64, axis=1) * sin


def chunk_y(y, j):
    return lax.rem(y + (0, 3, 1, 2)[j], 4)


def fill_rows(rows, own, before, after, far_a, far_b):
    rows[pl.ds(0, CHUNK), :] = own[...]
    rows[pl.ds(CHUNK, CHUNK), :] = before[...]
    rows[pl.ds(2 * CHUNK, CHUNK), :] = after[...]
    rows[pl.ds(3 * CHUNK, CHUNK // 2), :] = far_a[...]
    rows[pl.ds(3 * CHUNK + CHUNK // 2, CHUNK // 2), :] = far_b[...]


def kv_kernel(meta, own, before, after, far_a, far_b, wk, wv, bk, bv, cos_ref, sin_ref, out, rows):
    y = meta[0]
    fill_rows(rows, own, before, after, far_a, far_b)
    w = jnp.concatenate([wk[...], wv[...]], axis=1)
    both = jnp.dot(rows[...], w, preferred_element_type=jnp.float32)
    key_bias = bk[...]
    value_bias = bv[...]
    for j in range(4):
        base = pl.multiple_of(chunk_y(y, j) * 16, 16)
        cos = cos_ref[pl.ds(base, 16), :]
        sin = sin_ref[pl.ds(base, 16), :]
        for i in range(RESP):
            part = both[j * CHUNK + i * 16 : j * CHUNK + i * 16 + 16, :]
            key = rope(part[:, :HD] + key_bias, cos, sin).astype(jnp.bfloat16)
            value = (part[:, HD:] + value_bias).astype(jnp.bfloat16)
            out[i, pl.ds(base, 16), 0:HD] = key
            out[i, pl.ds(base, 16), HD : 2 * HD] = value


def own_keys_values(meta, chunks, w_key, w_value, b_key, b_value, cos, sin):
    whole = lambda shape: pl.BlockSpec(shape, lambda s, m: (0,) * len(shape))
    column = lambda rows: pl.BlockSpec((rows, HD), lambda s, m: (0, m[0]))
    return pl.pallas_call(
        kv_kernel,
        out_shape=jax.ShapeDtypeStruct((RESP, 64, 2 * HD), jnp.bfloat16),
        grid_spec=pltpu.PrefetchScalarGridSpec(
            num_scalar_prefetch=1,
            grid=(1,),
            in_specs=[whole(c.shape) for c in chunks]
            + [column(D), column(D), column(1), column(1), whole((64, HD)), whole((64, HD))],
            out_specs=whole((RESP, 64, 2 * HD)),
            scratch_shapes=[pltpu.VMEM((4 * CHUNK, D), jnp.bfloat16)],
        ),
        compiler_params=params(),
        name="keys_values",
    )(meta, *chunks, w_key, w_value, b_key, b_value, cos, sin)


def query_kernel(
    meta, own, before, after, far_a, far_b, w_mine, w_other, cos_ref, sin_ref, c_mine, c_other,
    q_out, acc_out, stat_out, rows,
):
    y = meta[0]
    c = meta[1]
    fill_rows(rows, own, before, after, far_a, far_b)
    mine_at = pl.multiple_of(c * HALF_D, 128)
    other_at = pl.multiple_of((1 - c) * HALF_D, 128)
    for pair in range(2):
        lo, hi = 2 * pair, 2 * pair + 1
        wm = jnp.concatenate([w_mine[lo, :HALF_D, :], w_mine[hi, :HALF_D, :]], axis=1)
        wo = jnp.concatenate([w_other[lo, :HALF_D, :], w_other[hi, :HALF_D, :]], axis=1)
        both = jnp.dot(rows[:, pl.ds(mine_at, HALF_D)], wm, preferred_element_type=jnp.float32)
        both = both + jnp.dot(rows[:, pl.ds(other_at, HALF_D)], wo, preferred_element_type=jnp.float32)
        for h in (lo, hi):
            tail = w_mine[h, HALF_D : HALF_D + BIAS_ROWS, :].astype(jnp.float32)
            bias = tail[0:1, :] + tail[1:2, :] + tail[2:3, :]
            raw = both[:, (h - lo) * HD : (h - lo + 1) * HD] + bias
            for j in range(4):
                base = pl.multiple_of(chunk_y(y, j) * 16, 16)
                cos = cos_ref[pl.ds(base, 16), :]
                sin = sin_ref[pl.ds(base, 16), :]
                for i in range(RESP):
                    part = raw[j * CHUNK + i * 16 : j * CHUNK + i * 16 + 16, :]
                    q_out[i, h, pl.ds(base, 16), :] = rope(part, cos, sin).astype(jnp.bfloat16)

    def step(i, carry):
        q = q_out[i].reshape(4 * 64, HD)
        keys = jnp.concatenate([c_mine[:, :HD], c_other[:, :HD]], axis=0)
        scores = lax.dot_general(q, keys, (((1,), (1,)), ((), ())), preferred_element_type=jnp.float32)
        top = jnp.max(scores, axis=-1, keepdims=True)
        weights = jnp.exp2(scores * (SCALE * LOG2E) - top * (SCALE * LOG2E))
        total = jnp.sum(weights, axis=-1, keepdims=True)
        values = jnp.concatenate([c_mine[:, HD:], c_other[:, HD:]], axis=0)
        acc_out[i] = jnp.dot(weights.astype(jnp.bfloat16), values, preferred_element_type=jnp.float32)
        lane = lax.broadcasted_iota(jnp.int32, (4 * 64, HD), 1)
        stat_out[i] = jnp.where(lane < 64, top, total)
        return carry

    lax.fori_loop(0, RESP, step, 0)


def rubric_part(meta, chunks, w_mine, w_other, cos, sin, c_mine, c_other):
    return pl.pallas_call(
        query_kernel,
        out_shape=(
            jax.ShapeDtypeStruct((RESP, 4, 64, HD), jnp.bfloat16),
            jax.ShapeDtypeStruct((RESP, 256, HD), jnp.float32),
            jax.ShapeDtypeStruct((RESP, 256, HD), jnp.float32),
        ),
        in_specs=[SMEM_SPEC] + [VMEM_SPEC] * 11,
        out_specs=(VMEM_SPEC, VMEM_SPEC, VMEM_SPEC),
        scratch_shapes=[pltpu.VMEM((4 * CHUNK, D), jnp.bfloat16)],
        compiler_params=params(),
        cost_estimate=pl.CostEstimate(
            flops=3_000_000_000, bytes_accessed=12_000_000, transcendentals=3_200_000
        ),
        name="rubric_part",
    )(meta, *chunks, w_mine, w_other, cos, sin, c_mine, c_other)


def self_kernel(meta, dest, lengths, q_ref, acc_ref, stat_ref, kv0, kv1, kv2, kv3, out):
    x = meta[2]
    g = meta[3]
    out[...] = jnp.zeros_like(out)
    row = lax.broadcasted_iota(jnp.int32, (256, 256), 0)
    col = lax.broadcasted_iota(jnp.int32, (256, 256), 1)
    slot_row = lax.rem(row, 64)
    row_pos = (slot_row // 16) * 64 + x * 16 + lax.rem(slot_row, 16)
    slot_col = lax.rem(col, 64)
    which = col // 64
    offset = jnp.where(which == 0, 0, jnp.where(which == 1, 3, jnp.where(which == 2, 1, 2)))
    col_x = lax.rem(x + offset, 4)
    col_pos = (slot_col // 16) * 64 + col_x * 16 + lax.rem(slot_col, 16)
    causal = col_pos <= row_pos
    one_pos = row_pos[:, 0:HD]
    for i in range(RESP):
        length = lengths[g * RESP + i]
        q = q_ref[i].reshape(256, HD)
        keys = jnp.concatenate([kv0[i, :, :HD], kv1[i, :, :HD], kv2[i, :, :HD], kv3[i, :, :HD]], axis=0)
        values = jnp.concatenate([kv0[i, :, HD:], kv1[i, :, HD:], kv2[i, :, HD:], kv3[i, :, HD:]], axis=0)
        scores = lax.dot_general(q, keys, (((1,), (1,)), ((), ())), preferred_element_type=jnp.float32)
        scores = jnp.where(causal & (col_pos < length), scores, -jnp.inf)
        far_top = stat_ref[i, :, 0:1]
        far_total = stat_ref[i, :, 64:65]
        top = jnp.maximum(jnp.max(scores, axis=-1, keepdims=True), far_top)
        weights = jnp.exp2((scores - top) * (SCALE * LOG2E))
        factor = jnp.exp2((far_top - top) * (SCALE * LOG2E))
        total = jnp.sum(weights, axis=-1, keepdims=True) + far_total * factor
        near = jnp.dot(weights.astype(jnp.bfloat16), values, preferred_element_type=jnp.float32)
        mixed = (acc_ref[i] * factor + near) / total
        mixed = jnp.where(one_pos < length, mixed, 0.0).astype(jnp.bfloat16)
        out[dest[g * RESP + i]] = mixed.reshape(4, 64, HD)


def self_part(meta, dest, lengths, q, acc, stat, parts):
    return pl.pallas_call(
        self_kernel,
        out_shape=jax.ShapeDtypeStruct((GROUPS, 4, 64, HD), jnp.bfloat16),
        in_specs=[SMEM_SPEC] * 3 + [VMEM_SPEC] * 7,
        out_specs=VMEM_SPEC,
        compiler_params=params(),
        name="self_part",
    )(meta, dest, lengths, q, acc, stat, *parts)


def on_device(
    tokens, gain, w_query, b_query, w_key, b_key, w_value, b_value, rubric_cache, dest_of, lengths
):
    g = lax.axis_index("score")
    m = lax.axis_index("mp")
    z, c = g // 2, g % 2
    y, x = m // 4, m % 4
    meta = jnp.stack([y, c, x, g]).astype(jnp.int32)

    normed = norm_rows(tokens.reshape(CHUNK, D), gain.reshape(1, D))
    before = shift(normed, dy=1)
    after = shift(normed, dy=-1)

    first = lax.reduce_precision(b_query, 8, 7)
    second = lax.reduce_precision(b_query - first, 8, 7)
    third = b_query - first - second
    tail = jnp.stack([first, second, third]).astype(jnp.bfloat16)
    tail = jnp.pad(tail, ((0, BIAS_ROWS - 3), (0, 0)))
    half = jnp.concatenate([lax.dynamic_slice_in_dim(w_query, c * HALF_D, HALF_D, 0), tail], axis=0)
    w_mine = lax.all_gather(half, "mp", axis=0, axis_index_groups=X_GROUPS)

    owner = dest_of[0]
    cache = rubric_cache[0]
    swapped = shift(cache, flip=1)
    cache = jnp.where(owner % 2 == c, cache, swapped)
    piece = lax.dynamic_slice_in_dim(cache, c * 64, 64, 1)
    piece, _ = lax.optimization_barrier((piece, normed))
    z_before = shift(piece, dz=1)
    z_after = shift(piece, dz=-1)
    z_far = shift(piece, dz=2)
    turn = (owner // 2 - z) % 4
    piece = jnp.where(
        turn == 0, piece, jnp.where(turn == 3, z_before, jnp.where(turn == 1, z_after, z_far))
    )
    spread = jnp.broadcast_to(piece[:, None], (4, 4, 64, 2 * HD)).reshape(16, 64, 2 * HD)
    before_then, after_then, _ = lax.optimization_barrier((before, after, spread))
    far_a = shift(before_then[: CHUNK // 2], dy=1)
    far_b = shift(after_then[CHUNK // 2 :], dy=-1)
    chunks = (normed, before, after, far_a, far_b)
    c_mine = lax.all_to_all(spread, "mp", 0, 0, tiled=True).reshape(1024, 2 * HD)
    c_other = shift(c_mine, flip=1)
    w_mine, _, _, _ = lax.optimization_barrier((w_mine, far_a, far_b, c_mine))
    w_other = shift(w_mine, flip=1)

    frequency = jnp.exp(jnp.arange(64, dtype=jnp.float32) * (-2.0 * math.log(THETA) / HD))
    slot = jnp.arange(64, dtype=jnp.int32)
    positions = PROMPT + (slot // 16) * 64 + x * 16 + slot % 16
    angles = positions.astype(jnp.float32)[:, None] * frequency[None, :]
    cos = jnp.cos(angles)
    sin = jnp.sin(angles)
    cos = jnp.concatenate([cos, cos], axis=1)
    sin = jnp.concatenate([-sin, sin], axis=1)

    kv = own_keys_values(
        meta, chunks, w_key, w_value, b_key.reshape(1, -1), b_value.reshape(1, -1), cos, sin
    )
    parts = (kv, shift(kv, dx=1), shift(kv, dx=-1), shift(kv, dx=2))
    q, acc, stat = rubric_part(meta, chunks, w_mine, w_other, cos, sin, c_mine, c_other)
    ready = self_part(meta, dest_of, lengths, q, acc, stat, parts)
    arrived = lax.all_to_all(
        ready.reshape(32, 64, HD), AXES, 0, 0, tiled=True, axis_index_groups=SCORE_X_GROUPS
    )
    result = arrived.reshape(GROUPS, 4, 4, 16, HD).transpose(0, 2, 1, 3, 4)
    return result.reshape(1, GROUPS, LEN_MAX, HD)


def solution(mesh):
    in_specs = (
        P("score", "mp", None),
        P(),
        P(None, "mp"),
        P("mp"),
        P(),
        P(),
        P(),
        P(),
        P("score", None, "mp", None),
        P(),
        P(),
    )
    out_specs = P("score", None, None, "mp")
    return jax.shard_map(
        on_device, mesh=mesh, in_specs=in_specs, out_specs=out_specs, check_vma=False
    )
```

```python
import math

import jax
import jax.numpy as jnp
from jax import lax
from jax.experimental import pallas as pl
from jax.experimental.pallas import tpu as pltpu
from jax.sharding import PartitionSpec as P

D = 3584
KV_HEADS = 4
HD = 128
LEN_MAX = 256
PROMPT = 2048
RESP = 6
GROUPS = 8
HALF_D = D // 2
BIAS_ROWS = 16
CHUNK = RESP * 16
THETA = 1000000.0
EPSILON = 1e-06
SCALE = 1.0 / math.sqrt(HD)
LIMIT = 36
LOG2E = math.log2(math.e)
AXES = ("score", "mp")


def device_number(x, y, z, c):
    return (z * 2 + c) * 16 + y * 4 + x


def shift(v, dx=0, dy=0, dz=0, flip=0):
    pairs = []
    for x in range(4):
        for y in range(4):
            for z in range(4):
                for c in range(2):
                    target = device_number((x + dx) % 4, (y + dy) % 4, (z + dz) % 4, c ^ flip)
                    pairs.append((device_number(x, y, z, c), target))
    return lax.ppermute(v, AXES, pairs)


def exchange_z(v, bit):
    pairs = []
    for x in range(4):
        for y in range(4):
            for z in range(4):
                for c in range(2):
                    pairs.append((device_number(x, y, z, c), device_number(x, y, z ^ bit, c)))
    return lax.ppermute(v, AXES, pairs)


SCORE_X_GROUPS = [[s * 16 + y * 4 + x for s in range(8) for x in range(4)] for y in range(4)]


def params(mib):
    return pltpu.CompilerParams(vmem_limit_bytes=mib * 1024 * 1024)


VMEM_SPEC = pl.BlockSpec(memory_space=pltpu.VMEM)
SMEM_SPEC = pl.BlockSpec(memory_space=pltpu.SMEM)


def rope(v, cos, sin):
    return v * cos + pltpu.roll(v, 64, axis=1) * sin


TURNS = (0, 3, 1, 2)


def chunk_y(y, j):
    return lax.rem(y + TURNS[j], 4)


def norm(tokens, gain):
    wide = tokens.astype(jnp.float32)
    mean = jnp.mean(wide * wide, axis=-1, keepdims=True)
    return (wide * lax.rsqrt(mean + EPSILON) * gain).astype(jnp.bfloat16)


def table(ref, y):
    base = pl.multiple_of(y * 16, 16)
    return base, ref[pl.ds(base, 16), :]


def project(y, rows, chunk_ids, wk, wv, bk, bv, cos_ref, sin_ref, out):
    w = jnp.concatenate([wk[...], wv[...]], axis=1)
    both = jnp.dot(rows, w, preferred_element_type=jnp.float32)
    at = pl.multiple_of(y * HD, HD)
    key = both[:, :HD] + bk[:, pl.ds(at, HD)]
    value = (both[:, HD:] + bv[:, pl.ds(at, HD)]).astype(jnp.bfloat16)
    for n, j in enumerate(chunk_ids):
        base, cos = table(cos_ref, chunk_y(y, j))
        ignored, sin = table(sin_ref, chunk_y(y, j))
        for i in range(RESP):
            part = slice(n * CHUNK + i * 16, n * CHUNK + i * 16 + 16)
            out[i, pl.ds(base, 16), 0:HD] = rope(key[part], cos, sin).astype(jnp.bfloat16)
            out[i, pl.ds(base, 16), HD : 2 * HD] = value[part]


def own_kernel(own, gain, rows):
    rows[...] = norm(own[...], gain[...])


def near_kernel(meta, own, before, after, gain, wk, wv, bk, bv, cos_ref, sin_ref, out, rows):
    out[...] = jnp.zeros_like(out)
    rows[0:CHUNK, :] = own[...]
    rows[CHUNK : 2 * CHUNK, :] = norm(before[...], gain[...])
    rows[2 * CHUNK : 3 * CHUNK, :] = norm(after[...], gain[...])
    project(meta[0], rows[...], (0, 1, 2), wk, wv, bk, bv, cos_ref, sin_ref, out)


def far_kernel(meta, near, far_a, far_b, gain, wk, wv, bk, bv, cos_ref, sin_ref, out, rows):
    out[...] = near[...]
    rows[0 : CHUNK // 2, :] = norm(far_a[...], gain[...])
    rows[CHUNK // 2 : CHUNK, :] = norm(far_b[...], gain[...])
    project(meta[0], rows[...], (3,), wk, wv, bk, bv, cos_ref, sin_ref, out)


def norm_own(own, gain):
    return pl.pallas_call(
        own_kernel,
        out_shape=jax.ShapeDtypeStruct((CHUNK, D), jnp.bfloat16),
        in_specs=[VMEM_SPEC] * 2,
        out_specs=VMEM_SPEC,
        compiler_params=params(LIMIT),
        name="own_rows",
    )(own, gain)


def keys_values(kernel, name, count, meta, chunks, small):
    return pl.pallas_call(
        kernel,
        out_shape=(
            jax.ShapeDtypeStruct((RESP, 64, 2 * HD), jnp.bfloat16),
            jax.ShapeDtypeStruct((count, D), jnp.bfloat16),
        ),
        in_specs=[SMEM_SPEC] + [VMEM_SPEC] * (len(chunks) + len(small)),
        out_specs=(VMEM_SPEC, VMEM_SPEC),
        compiler_params=params(LIMIT),
        name=name,
    )(meta, *chunks, *small)


def query_kernel(
    meta, near, far, w_own, b_own, m1, m2, m3, o1, o2, o3, cos_ref, sin_ref, q_out, rows
):
    y, c, x = meta[0], meta[1], meta[2]
    rows[0 : 3 * CHUNK, :] = near[...]
    rows[3 * CHUNK : 4 * CHUNK, :] = far[...]
    mine_at = pl.multiple_of(c * HALF_D, 128)
    other_at = pl.multiple_of((1 - c) * HALF_D, 128)

    def bias(ref):
        tail = ref[HALF_D : HALF_D + BIAS_ROWS, :].astype(jnp.float32)
        return tail[0:1, :] + tail[1:2, :] + tail[2:3, :]

    mine = [w_own[pl.ds(mine_at, HALF_D), :]] + [ref[:HALF_D, :] for ref in (m1, m2, m3)]
    other = [w_own[pl.ds(other_at, HALF_D), :]] + [ref[:HALF_D, :] for ref in (o1, o2, o3)]
    biases = [b_own[...], bias(m1), bias(m2), bias(m3)]
    for lo in (0, 2):
        first = jnp.concatenate(mine[lo : lo + 2], axis=1)
        second = jnp.concatenate(other[lo : lo + 2], axis=1)
        both = jnp.dot(rows[:, pl.ds(mine_at, HALF_D)], first, preferred_element_type=jnp.float32)
        both = both + jnp.dot(
            rows[:, pl.ds(other_at, HALF_D)], second, preferred_element_type=jnp.float32
        )
        for n in (lo, lo + 1):
            head = lax.rem(x + TURNS[n], 4)
            raw = both[:, (n - lo) * HD : (n - lo + 1) * HD] + biases[n]
            for j in range(4):
                base, cos = table(cos_ref, chunk_y(y, j))
                ignored, sin = table(sin_ref, chunk_y(y, j))
                for i in range(RESP):
                    part = raw[j * CHUNK + i * 16 : j * CHUNK + i * 16 + 16, :]
                    q_out[i, head, pl.ds(base, 16), :] = rope(part, cos, sin).astype(jnp.bfloat16)


def make_queries(meta, near, far, w_own, b_own, mine, other, cos, sin):
    return pl.pallas_call(
        query_kernel,
        out_shape=jax.ShapeDtypeStruct((RESP, 4, 64, HD), jnp.bfloat16),
        in_specs=[SMEM_SPEC] + [VMEM_SPEC] * 12,
        out_specs=VMEM_SPEC,
        scratch_shapes=[pltpu.VMEM((4 * CHUNK, D), jnp.bfloat16)],
        compiler_params=params(LIMIT),
        name="queries",
    )(meta, near, far, w_own, b_own, *mine, *other, cos, sin)


def rubric_kernel(q_ref, c_mine, c_other, acc_out, stat_out):
    def step(i, carry):
        q = q_ref[i].reshape(4 * 64, HD)
        keys = jnp.concatenate([c_mine[:, :HD], c_other[:, :HD]], axis=0)
        scores = lax.dot_general(q, keys, (((1,), (1,)), ((), ())), preferred_element_type=jnp.float32)
        top = jnp.max(scores, axis=-1, keepdims=True)
        weights = jnp.exp2(scores * (SCALE * LOG2E) - top * (SCALE * LOG2E))
        total = jnp.sum(weights, axis=-1, keepdims=True)
        values = jnp.concatenate([c_mine[:, HD:], c_other[:, HD:]], axis=0)
        acc_out[i] = jnp.dot(weights.astype(jnp.bfloat16), values, preferred_element_type=jnp.float32)
        lane = lax.broadcasted_iota(jnp.int32, (4 * 64, HD), 1)
        stat_out[i] = jnp.where(lane < 64, top, total)
        return carry

    lax.fori_loop(0, RESP, step, 0)


def rubric_part(q, c_mine, c_other):
    return pl.pallas_call(
        rubric_kernel,
        out_shape=(
            jax.ShapeDtypeStruct((RESP, 256, HD), jnp.float32),
            jax.ShapeDtypeStruct((RESP, 256, HD), jnp.float32),
        ),
        in_specs=[VMEM_SPEC] * 3,
        out_specs=(VMEM_SPEC, VMEM_SPEC),
        compiler_params=params(LIMIT),
        name="rubric_part",
    )(q, c_mine, c_other)


def self_kernel(meta, dest, lengths, q_ref, acc_ref, stat_ref, kv0, kv1, kv2, kv3, out):
    x = meta[2]
    g = meta[3]
    out[...] = jnp.zeros_like(out)
    row = lax.broadcasted_iota(jnp.int32, (256, 256), 0)
    col = lax.broadcasted_iota(jnp.int32, (256, 256), 1)
    slot_row = lax.rem(row, 64)
    row_pos = (slot_row // 16) * 64 + x * 16 + lax.rem(slot_row, 16)
    slot_col = lax.rem(col, 64)
    which = col // 64
    offset = jnp.where(which == 0, 0, jnp.where(which == 1, 3, jnp.where(which == 2, 1, 2)))
    col_x = lax.rem(x + offset, 4)
    col_pos = (slot_col // 16) * 64 + col_x * 16 + lax.rem(slot_col, 16)
    causal = col_pos <= row_pos
    one_pos = row_pos[:, 0:HD]
    for i in range(RESP):
        length = lengths[g * RESP + i]
        q = q_ref[i].reshape(256, HD)
        keys = jnp.concatenate([kv0[i, :, :HD], kv1[i, :, :HD], kv2[i, :, :HD], kv3[i, :, :HD]], axis=0)
        values = jnp.concatenate([kv0[i, :, HD:], kv1[i, :, HD:], kv2[i, :, HD:], kv3[i, :, HD:]], axis=0)
        scores = lax.dot_general(q, keys, (((1,), (1,)), ((), ())), preferred_element_type=jnp.float32)
        scores = jnp.where(causal & (col_pos < length), scores, -jnp.inf)
        far_top = stat_ref[i, :, 0:1]
        far_total = stat_ref[i, :, 64:65]
        top = jnp.maximum(jnp.max(scores, axis=-1, keepdims=True), far_top)
        weights = jnp.exp2((scores - top) * (SCALE * LOG2E))
        factor = jnp.exp2((far_top - top) * (SCALE * LOG2E))
        total = jnp.sum(weights, axis=-1, keepdims=True) + far_total * factor
        near = jnp.dot(weights.astype(jnp.bfloat16), values, preferred_element_type=jnp.float32)
        mixed = (acc_ref[i] * factor + near) / total
        mixed = jnp.where(one_pos < length, mixed, 0.0).astype(jnp.bfloat16)
        out[dest[g * RESP + i]] = mixed.reshape(4, 64, HD)


def self_part(meta, dest, lengths, q, acc, stat, parts):
    return pl.pallas_call(
        self_kernel,
        out_shape=jax.ShapeDtypeStruct((GROUPS, 4, 64, HD), jnp.bfloat16),
        in_specs=[SMEM_SPEC] * 3 + [VMEM_SPEC] * 7,
        out_specs=VMEM_SPEC,
        compiler_params=params(LIMIT),
        name="self_part",
    )(meta, dest, lengths, q, acc, stat, *parts)


def on_device(
    tokens, gain, w_query, b_query, w_key, b_key, w_value, b_value, rubric_cache, dest_of, lengths
):
    g = lax.axis_index("score")
    m = lax.axis_index("mp")
    z, c = g // 2, g % 2
    y, x = m // 4, m % 4
    meta = jnp.stack([y, c, x, g]).astype(jnp.int32)

    own = tokens.reshape(CHUNK, D)
    gain = gain.reshape(1, D)
    before = shift(own, dy=1)
    after = shift(own, dy=-1)
    far_a = shift(before[: CHUNK // 2], dy=1)
    far_b = shift(after[CHUNK // 2 :], dy=-1)

    frequency = jnp.exp(jnp.arange(64, dtype=jnp.float32) * (-2.0 * math.log(THETA) / HD))
    slot = jnp.arange(64, dtype=jnp.int32)
    positions = PROMPT + (slot // 16) * 64 + x * 16 + slot % 16
    angles = positions.astype(jnp.float32)[:, None] * frequency[None, :]
    cos = jnp.cos(angles)
    sin = jnp.sin(angles)
    cos = jnp.concatenate([cos, cos], axis=1)
    sin = jnp.concatenate([-sin, sin], axis=1)

    wk = lax.dynamic_slice_in_dim(w_key, y * HD, HD, 1)
    wv = lax.dynamic_slice_in_dim(w_value, y * HD, HD, 1)
    small = (gain, wk, wv, b_key.reshape(1, -1), b_value.reshape(1, -1), cos, sin)
    own_rows = norm_own(own, gain)

    first = lax.reduce_precision(b_query, 8, 7)
    second = lax.reduce_precision(b_query - first, 8, 7)
    third = b_query - first - second
    tail = jnp.stack([first, second, third]).astype(jnp.bfloat16)
    tail = jnp.pad(tail, ((0, BIAS_ROWS - 3), (0, 0)))
    half = jnp.concatenate([lax.dynamic_slice_in_dim(w_query, c * HALF_D, HALF_D, 0), tail], axis=0)
    mine = (shift(half, dx=1), shift(half, dx=-1), shift(half, dx=2))
    other = tuple(shift(v, flip=1) for v in mine)

    owner = dest_of[0]
    cache = rubric_cache[0]
    swapped = shift(cache, flip=1)
    cache = jnp.where(owner % 2 == c, cache, swapped)
    piece = lax.dynamic_slice_in_dim(cache, c * 64, 64, 1)
    for bit in (1, 2):
        across = exchange_z(piece, bit)
        same = (owner // 2 & bit) == (z & bit)
        piece = jnp.where(same, piece, across)
    spread = jnp.broadcast_to(piece[:, None], (4, 4, 64, 2 * HD)).reshape(16, 64, 2 * HD)
    c_mine = lax.all_to_all(spread, "mp", 0, 0, tiled=True).reshape(1024, 2 * HD)

    kv, near_rows = keys_values(
        near_kernel, "near_rows", 3 * CHUNK, meta, (own_rows, before, after), small
    )
    c_mine, _ = lax.optimization_barrier((c_mine, near_rows))
    c_other = shift(c_mine, flip=1)
    kv, far_rows = keys_values(far_kernel, "far_rows", CHUNK, meta, (kv, far_a, far_b), small)
    parts = (kv, shift(kv, dx=1), shift(kv, dx=-1), shift(kv, dx=2))
    q = make_queries(
        meta, near_rows, far_rows, w_query, b_query.reshape(1, HD), mine, other, cos, sin
    )
    acc, stat = rubric_part(q, c_mine, c_other)
    ready = self_part(meta, dest_of, lengths, q, acc, stat, parts)
    arrived = lax.all_to_all(
        ready.reshape(32, 64, HD), AXES, 0, 0, tiled=True, axis_index_groups=SCORE_X_GROUPS
    )
    result = arrived.reshape(GROUPS, 4, 4, 16, HD).transpose(0, 2, 1, 3, 4)
    return result.reshape(1, GROUPS, LEN_MAX, HD)


def solution(mesh):
    in_specs = (
        P("score", "mp", None),
        P(),
        P(None, "mp"),
        P("mp"),
        P(),
        P(),
        P(),
        P(),
        P("score", None, "mp", None),
        P(),
        P(),
    )
    out_specs = P("score", None, None, "mp")
    return jax.shard_map(
        on_device, mesh=mesh, in_specs=in_specs, out_specs=out_specs, check_vma=False
    )
```

```python
import math

import jax
import jax.numpy as jnp
from jax import lax
from jax.experimental import pallas as pl
from jax.experimental.pallas import tpu as pltpu
from jax.sharding import PartitionSpec as P

D = 3584
KV_HEADS = 4
HD = 128
LEN_MAX = 256
PROMPT = 2048
RESP = 6
GROUPS = 8
BIAS_ROWS = 16
CHUNK = RESP * 16
THETA = 1000000.0
EPSILON = 1e-06
SCALE = 1.0 / math.sqrt(HD)
LIMIT = 36
LOG2E = math.log2(math.e)
AXES = ("score", "mp")


def device_number(x, y, z, c):
    return (z * 2 + c) * 16 + y * 4 + x


def shift(v, dx=0, dy=0, dz=0, flip=0):
    pairs = []
    for x in range(4):
        for y in range(4):
            for z in range(4):
                for c in range(2):
                    target = device_number((x + dx) % 4, (y + dy) % 4, (z + dz) % 4, c ^ flip)
                    pairs.append((device_number(x, y, z, c), target))
    return lax.ppermute(v, AXES, pairs)


def both_ways(v, axis):
    pairs = []
    for x in range(4):
        for y in range(4):
            for z in range(4):
                for c in range(2):
                    at = {"x": x, "y": y, "z": z}
                    at[axis] = (at[axis] + 1 - 2 * c) % 4
                    pairs.append((device_number(x, y, z, c), device_number(**at, c=c)))
    return lax.ppermute(v, AXES, pairs)


SCORE_X_GROUPS = [[s * 16 + y * 4 + x for s in range(8) for x in range(4)] for y in range(4)]


def params(mib):
    return pltpu.CompilerParams(vmem_limit_bytes=mib * 1024 * 1024)


VMEM_SPEC = pl.BlockSpec(memory_space=pltpu.VMEM)
SMEM_SPEC = pl.BlockSpec(memory_space=pltpu.SMEM)


def rope(v, cos, sin):
    return v * cos + pltpu.roll(v, 64, axis=1) * sin


TURNS = (0, 3, 1, 2)


def chunk_y(y, j):
    return lax.rem(y + TURNS[j], 4)


def norm(tokens, gain):
    wide = tokens.astype(jnp.float32)
    mean = jnp.mean(wide * wide, axis=-1, keepdims=True)
    return (wide * lax.rsqrt(mean + EPSILON) * gain).astype(jnp.bfloat16)


def table(ref, y):
    base = pl.multiple_of(y * 16, 16)
    return base, ref[pl.ds(base, 16), :]


def project(y, rows, chunk_ids, wk, wv, bk, bv, cos_ref, sin_ref, out):
    w = jnp.concatenate([wk[...], wv[...]], axis=1)
    both = jnp.dot(rows, w, preferred_element_type=jnp.float32)
    at = pl.multiple_of(y * HD, HD)
    key = both[:, :HD] + bk[:, pl.ds(at, HD)]
    value = (both[:, HD:] + bv[:, pl.ds(at, HD)]).astype(jnp.bfloat16)
    for n, j in enumerate(chunk_ids):
        base, cos = table(cos_ref, chunk_y(y, j))
        ignored, sin = table(sin_ref, chunk_y(y, j))
        for i in range(RESP):
            part = slice(n * CHUNK + i * 16, n * CHUNK + i * 16 + 16)
            out[i, pl.ds(base, 16), 0:HD] = rope(key[part], cos, sin).astype(jnp.bfloat16)
            out[i, pl.ds(base, 16), HD : 2 * HD] = value[part]


def near_kernel(meta, own, before, after, gain, wk, wv, bk, bv, cos_ref, sin_ref, out, rows):
    out[...] = jnp.zeros_like(out)
    rows[0:CHUNK, :] = norm(own[...], gain[...])
    rows[CHUNK : 2 * CHUNK, :] = norm(before[...], gain[...])
    rows[2 * CHUNK : 3 * CHUNK, :] = norm(after[...], gain[...])
    project(meta[0], rows[...], (0, 1, 2), wk, wv, bk, bv, cos_ref, sin_ref, out)


def far_kernel(meta, near, far, gain, wk, wv, bk, bv, cos_ref, sin_ref, out, rows):
    out[...] = near[...]
    rows[...] = norm(far[...], gain[...])
    project(meta[0], rows[...], (3,), wk, wv, bk, bv, cos_ref, sin_ref, out)


def keys_values(kernel, name, count, meta, chunks, small):
    return pl.pallas_call(
        kernel,
        out_shape=(
            jax.ShapeDtypeStruct((RESP, 64, 2 * HD), jnp.bfloat16),
            jax.ShapeDtypeStruct((count, D), jnp.bfloat16),
        ),
        in_specs=[SMEM_SPEC] + [VMEM_SPEC] * (len(chunks) + len(small)),
        out_specs=(VMEM_SPEC, VMEM_SPEC),
        compiler_params=params(LIMIT),
        name=name,
    )(meta, *chunks, *small)


def query_kernel(meta, near, far, w0, w1, w2, w3, cos_ref, sin_ref, q_out, rows):
    y, c, x = meta[0], meta[1], meta[2]
    rows[0 : 3 * CHUNK, :] = near[...]
    rows[3 * CHUNK : 4 * CHUNK, :] = far[...]
    weights = (w0, w1, w2, w3)
    heads = [lax.rem(x + turn, 4) for turn in (0, 3 - 2 * c, 1 + 2 * c, 2)]
    for lo in (0, 2):
        w = jnp.concatenate([weights[lo][:D, :], weights[lo + 1][:D, :]], axis=1)
        both = jnp.dot(rows[...], w, preferred_element_type=jnp.float32)
        for n in (lo, lo + 1):
            tail = weights[n][D : D + BIAS_ROWS, :].astype(jnp.float32)
            bias = tail[0:1, :] + tail[1:2, :] + tail[2:3, :]
            raw = both[:, (n - lo) * HD : (n - lo + 1) * HD] + bias
            for j in range(4):
                base, cos = table(cos_ref, chunk_y(y, j))
                ignored, sin = table(sin_ref, chunk_y(y, j))
                for i in range(RESP):
                    part = raw[j * CHUNK + i * 16 : j * CHUNK + i * 16 + 16, :]
                    rotated = rope(part, cos, sin).astype(jnp.bfloat16)
                    q_out[i, heads[n], pl.ds(base, 16), :] = rotated


def make_queries(meta, near, far, weights, cos, sin):
    return pl.pallas_call(
        query_kernel,
        out_shape=jax.ShapeDtypeStruct((RESP, 4, 64, HD), jnp.bfloat16),
        in_specs=[SMEM_SPEC] + [VMEM_SPEC] * 8,
        out_specs=VMEM_SPEC,
        scratch_shapes=[pltpu.VMEM((4 * CHUNK, D), jnp.bfloat16)],
        compiler_params=params(LIMIT),
        name="queries",
    )(meta, near, far, *weights, cos, sin)


def rubric_kernel(q_ref, c_mine, c_other, acc_out, stat_out):
    def step(i, carry):
        q = q_ref[i].reshape(4 * 64, HD)
        keys = jnp.concatenate([c_mine[:, :HD], c_other[:, :HD]], axis=0)
        scores = lax.dot_general(q, keys, (((1,), (1,)), ((), ())), preferred_element_type=jnp.float32)
        top = jnp.max(scores, axis=-1, keepdims=True)
        weights = jnp.exp2(scores * (SCALE * LOG2E) - top * (SCALE * LOG2E))
        total = jnp.sum(weights, axis=-1, keepdims=True)
        values = jnp.concatenate([c_mine[:, HD:], c_other[:, HD:]], axis=0)
        acc_out[i] = jnp.dot(weights.astype(jnp.bfloat16), values, preferred_element_type=jnp.float32)
        lane = lax.broadcasted_iota(jnp.int32, (4 * 64, HD), 1)
        stat_out[i] = jnp.where(lane < 64, top, total)
        return carry

    lax.fori_loop(0, RESP, step, 0, unroll=True)


def rubric_part(q, c_mine, c_other):
    return pl.pallas_call(
        rubric_kernel,
        out_shape=(
            jax.ShapeDtypeStruct((RESP, 256, HD), jnp.float32),
            jax.ShapeDtypeStruct((RESP, 256, HD), jnp.float32),
        ),
        in_specs=[VMEM_SPEC] * 3,
        out_specs=(VMEM_SPEC, VMEM_SPEC),
        compiler_params=params(LIMIT),
        name="rubric_part",
    )(q, c_mine, c_other)


def self_kernel(meta, dest, lengths, q_ref, acc_ref, stat_ref, kv0, kv1, kv2, kv3, out):
    x = meta[2]
    g = meta[3]
    out[...] = jnp.zeros_like(out)
    row = lax.broadcasted_iota(jnp.int32, (256, 256), 0)
    col = lax.broadcasted_iota(jnp.int32, (256, 256), 1)
    slot_row = lax.rem(row, 64)
    row_pos = (slot_row // 16) * 64 + x * 16 + lax.rem(slot_row, 16)
    slot_col = lax.rem(col, 64)
    which = col // 64
    offset = jnp.where(which == 0, 0, jnp.where(which == 1, 3, jnp.where(which == 2, 1, 2)))
    col_x = lax.rem(x + offset, 4)
    col_pos = (slot_col // 16) * 64 + col_x * 16 + lax.rem(slot_col, 16)
    causal = col_pos <= row_pos
    one_pos = row_pos[:, 0:HD]
    for i in range(RESP):
        length = lengths[g * RESP + i]
        q = q_ref[i].reshape(256, HD)
        keys = jnp.concatenate([kv0[i, :, :HD], kv1[i, :, :HD], kv2[i, :, :HD], kv3[i, :, :HD]], axis=0)
        values = jnp.concatenate([kv0[i, :, HD:], kv1[i, :, HD:], kv2[i, :, HD:], kv3[i, :, HD:]], axis=0)
        scores = lax.dot_general(q, keys, (((1,), (1,)), ((), ())), preferred_element_type=jnp.float32)
        scores = jnp.where(causal & (col_pos < length), scores, -jnp.inf)
        far_top = stat_ref[i, :, 0:1]
        far_total = stat_ref[i, :, 64:65]
        top = jnp.maximum(jnp.max(scores, axis=-1, keepdims=True), far_top)
        weights = jnp.exp2((scores - top) * (SCALE * LOG2E))
        factor = jnp.exp2((far_top - top) * (SCALE * LOG2E))
        total = jnp.sum(weights, axis=-1, keepdims=True) + far_total * factor
        near = jnp.dot(weights.astype(jnp.bfloat16), values, preferred_element_type=jnp.float32)
        mixed = (acc_ref[i] * factor + near) / total
        mixed = jnp.where(one_pos < length, mixed, 0.0).astype(jnp.bfloat16)
        out[dest[g * RESP + i]] = mixed.reshape(4, 64, HD)


def self_part(meta, dest, lengths, q, acc, stat, parts):
    return pl.pallas_call(
        self_kernel,
        out_shape=jax.ShapeDtypeStruct((GROUPS, 4, 64, HD), jnp.bfloat16),
        in_specs=[SMEM_SPEC] * 3 + [VMEM_SPEC] * 7,
        out_specs=VMEM_SPEC,
        compiler_params=params(LIMIT),
        name="self_part",
    )(meta, dest, lengths, q, acc, stat, *parts)


def on_device(
    tokens, gain, w_query, b_query, w_key, b_key, w_value, b_value, rubric_cache, dest_of, lengths
):
    g = lax.axis_index("score")
    m = lax.axis_index("mp")
    z, c = g // 2, g % 2
    y, x = m // 4, m % 4
    meta = jnp.stack([y, c, x, g]).astype(jnp.int32)

    own = tokens.reshape(CHUNK, D)
    gain = gain.reshape(1, D)
    before = shift(own, dy=1)
    after = shift(own, dy=-1)
    far = shift(own, dy=2)

    frequency = jnp.exp(jnp.arange(64, dtype=jnp.float32) * (-2.0 * math.log(THETA) / HD))
    slot = jnp.arange(64, dtype=jnp.int32)
    positions = PROMPT + (slot // 16) * 64 + x * 16 + slot % 16
    angles = positions.astype(jnp.float32)[:, None] * frequency[None, :]
    cos = jnp.cos(angles)
    sin = jnp.sin(angles)
    cos = jnp.concatenate([cos, cos], axis=1)
    sin = jnp.concatenate([-sin, sin], axis=1)

    wk = lax.dynamic_slice_in_dim(w_key, y * HD, HD, 1)
    wv = lax.dynamic_slice_in_dim(w_value, y * HD, HD, 1)
    small = (gain, wk, wv, b_key.reshape(1, -1), b_value.reshape(1, -1), cos, sin)

    first = lax.reduce_precision(b_query, 8, 7)
    second = lax.reduce_precision(b_query - first, 8, 7)
    third = b_query - first - second
    tail = jnp.stack([first, second, third]).astype(jnp.bfloat16)
    tail = jnp.pad(tail, ((0, BIAS_ROWS - 3), (0, 0)))
    w_own = jnp.concatenate([w_query, tail], axis=0)
    w_beside = both_ways(w_own, "x")
    w_across = shift(w_beside, flip=1)
    w_far = both_ways(w_beside, "x")

    owner = dest_of[0]
    cache = rubric_cache[0]
    swapped = shift(cache, flip=1)
    cache = jnp.where(owner % 2 == c, cache, swapped)
    beside = both_ways(cache, "z")
    across = shift(beside, flip=1)
    turn = (owner // 2 - z) % 4
    here = jnp.where(c == 0, 3, 1)
    cache = jnp.where(turn == here, beside, jnp.where(turn == 4 - here, across, cache))
    piece = lax.dynamic_slice_in_dim(cache, c * 64, 64, 1)
    piece = jnp.where(turn == 2, both_ways(piece, "z"), piece)
    spread = jnp.broadcast_to(piece[:, None], (4, 4, 64, 2 * HD)).reshape(16, 64, 2 * HD)
    c_mine = lax.all_to_all(spread, "mp", 0, 0, tiled=True).reshape(1024, 2 * HD)

    kv, near_rows = keys_values(
        near_kernel, "near_rows", 3 * CHUNK, meta, (own, before, after), small
    )
    kv, far_rows = keys_values(far_kernel, "far_rows", CHUNK, meta, (kv, far), small)
    c_mine, _ = lax.optimization_barrier((c_mine, kv))
    c_other = shift(c_mine, flip=1)
    parts = (kv, shift(kv, dx=1), shift(kv, dx=-1), shift(kv, dx=2))
    far_rows, _ = lax.optimization_barrier((far_rows, c_other))
    weights = (w_own, w_beside, w_across, w_far)
    q = make_queries(meta, near_rows, far_rows, weights, cos, sin)
    acc, stat = rubric_part(q, c_mine, c_other)
    ready = self_part(meta, dest_of, lengths, q, acc, stat, parts)
    arrived = lax.all_to_all(
        ready.reshape(32, 64, HD), AXES, 0, 0, tiled=True, axis_index_groups=SCORE_X_GROUPS
    )
    result = arrived.reshape(GROUPS, 4, 4, 16, HD).transpose(0, 2, 1, 3, 4)
    return result.reshape(1, GROUPS, LEN_MAX, HD)


def solution(mesh):
    in_specs = (
        P("score", "mp", None),
        P(),
        P(None, "mp"),
        P("mp"),
        P(),
        P(),
        P(),
        P(),
        P("score", None, "mp", None),
        P(),
        P(),
    )
    out_specs = P("score", None, None, "mp")
    return jax.shard_map(
        on_device, mesh=mesh, in_specs=in_specs, out_specs=out_specs, check_vma=False
    )
```

```python
import math

import jax
import jax.numpy as jnp
from jax import lax
from jax.experimental import pallas as pl
from jax.experimental.pallas import tpu as pltpu
from jax.sharding import PartitionSpec as P

D = 3584
KV_HEADS = 4
HD = 128
LEN_MAX = 256
PROMPT = 2048
RESP = 6
GROUPS = 8
BIAS_ROWS = 16
CHUNK = RESP * 16
THETA = 1000000.0
EPSILON = 1e-06
SCALE = 1.0 / math.sqrt(HD)
LIMIT = 36
LOG2E = math.log2(math.e)
AXES = ("score", "mp")


def device_number(x, y, z, c):
    return (z * 2 + c) * 16 + y * 4 + x


def shift(v, dx=0, dy=0, dz=0, flip=0):
    pairs = []
    for x in range(4):
        for y in range(4):
            for z in range(4):
                for c in range(2):
                    target = device_number((x + dx) % 4, (y + dy) % 4, (z + dz) % 4, c ^ flip)
                    pairs.append((device_number(x, y, z, c), target))
    return lax.ppermute(v, AXES, pairs)


def both_ways(v, axis, step=1):
    pairs = []
    for x in range(4):
        for y in range(4):
            for z in range(4):
                for c in range(2):
                    at = {"x": x, "y": y, "z": z}
                    at[axis] = (at[axis] + step * (1 - 2 * c)) % 4
                    pairs.append((device_number(x, y, z, c), device_number(**at, c=c)))
    return lax.ppermute(v, AXES, pairs)


SCORE_X_GROUPS = [[s * 16 + y * 4 + x for s in range(8) for x in range(4)] for y in range(4)]


def params(mib):
    return pltpu.CompilerParams(vmem_limit_bytes=mib * 1024 * 1024)


VMEM_SPEC = pl.BlockSpec(memory_space=pltpu.VMEM)
SMEM_SPEC = pl.BlockSpec(memory_space=pltpu.SMEM)


def rope(v, cos, sin):
    return v * cos + pltpu.roll(v, 64, axis=1) * sin


TURNS = (0, 3, 1, 2)


def chunk_y(y, j):
    return lax.rem(y + TURNS[j], 4)


def norm(tokens, gain):
    wide = tokens.astype(jnp.float32)
    mean = jnp.mean(wide * wide, axis=-1, keepdims=True)
    return (wide * lax.rsqrt(mean + EPSILON) * gain).astype(jnp.bfloat16)


def table(ref, y):
    base = pl.multiple_of(y * 16, 16)
    return base, ref[pl.ds(base, 16), :]


def project(y, rows, chunk_ids, wk, wv, bk, bv, cos_ref, sin_ref, out):
    w = jnp.concatenate([wk[...], wv[...]], axis=1)
    both = jnp.dot(rows, w, preferred_element_type=jnp.float32)
    at = pl.multiple_of(y * HD, HD)
    key = both[:, :HD] + bk[:, pl.ds(at, HD)]
    value = (both[:, HD:] + bv[:, pl.ds(at, HD)]).astype(jnp.bfloat16)
    for n, j in enumerate(chunk_ids):
        base, cos = table(cos_ref, chunk_y(y, j))
        ignored, sin = table(sin_ref, chunk_y(y, j))
        for i in range(RESP):
            part = slice(n * CHUNK + i * 16, n * CHUNK + i * 16 + 16)
            out[i, pl.ds(base, 16), 0:HD] = rope(key[part], cos, sin).astype(jnp.bfloat16)
            out[i, pl.ds(base, 16), HD : 2 * HD] = value[part]


def near_kernel(meta, own, before, after, gain, wk, wv, bk, bv, cos_ref, sin_ref, out, rows):
    out[...] = jnp.zeros_like(out)
    rows[0:CHUNK, :] = norm(own[...], gain[...])
    rows[CHUNK : 2 * CHUNK, :] = norm(before[...], gain[...])
    rows[2 * CHUNK : 3 * CHUNK, :] = norm(after[...], gain[...])
    project(meta[0], rows[...], (0, 1, 2), wk, wv, bk, bv, cos_ref, sin_ref, out)


def far_kernel(meta, near, far_a, far_b, gain, wk, wv, bk, bv, cos_ref, sin_ref, out, rows):
    out[...] = near[...]
    rows[0 : CHUNK // 2, :] = norm(far_a[...], gain[...])
    rows[CHUNK // 2 : CHUNK, :] = norm(far_b[...], gain[...])
    project(meta[0], rows[...], (3,), wk, wv, bk, bv, cos_ref, sin_ref, out)


def keys_values(kernel, name, count, meta, chunks, small):
    return pl.pallas_call(
        kernel,
        out_shape=(
            jax.ShapeDtypeStruct((RESP, 64, 2 * HD), jnp.bfloat16),
            jax.ShapeDtypeStruct((count, D), jnp.bfloat16),
        ),
        in_specs=[SMEM_SPEC] + [VMEM_SPEC] * (len(chunks) + len(small)),
        out_specs=(VMEM_SPEC, VMEM_SPEC),
        compiler_params=params(LIMIT),
        name=name,
    )(meta, *chunks, *small)


def query_kernel(meta, near, far, w0, w1, w2, w3, cos_ref, sin_ref, q_out, rows):
    y, c, x = meta[0], meta[1], meta[2]
    rows[0 : 3 * CHUNK, :] = near[...]
    rows[3 * CHUNK : 4 * CHUNK, :] = far[...]
    weights = (w0, w1, w2, w3)
    heads = [lax.rem(x + turn, 4) for turn in (0, 3 - 2 * c, 1 + 2 * c, 2)]
    for lo in (0, 2):
        w = jnp.concatenate([weights[lo][:D, :], weights[lo + 1][:D, :]], axis=1)
        both = jnp.dot(rows[...], w, preferred_element_type=jnp.float32)
        for n in (lo, lo + 1):
            tail = weights[n][D : D + BIAS_ROWS, :].astype(jnp.float32)
            bias = tail[0:1, :] + tail[1:2, :] + tail[2:3, :]
            raw = both[:, (n - lo) * HD : (n - lo + 1) * HD] + bias
            for j in range(4):
                base, cos = table(cos_ref, chunk_y(y, j))
                ignored, sin = table(sin_ref, chunk_y(y, j))
                for i in range(RESP):
                    part = raw[j * CHUNK + i * 16 : j * CHUNK + i * 16 + 16, :]
                    rotated = rope(part, cos, sin).astype(jnp.bfloat16)
                    q_out[i, heads[n], pl.ds(base, 16), :] = rotated


def make_queries(meta, near, far, weights, cos, sin):
    return pl.pallas_call(
        query_kernel,
        out_shape=jax.ShapeDtypeStruct((RESP, 4, 64, HD), jnp.bfloat16),
        in_specs=[SMEM_SPEC] + [VMEM_SPEC] * 8,
        out_specs=VMEM_SPEC,
        scratch_shapes=[pltpu.VMEM((4 * CHUNK, D), jnp.bfloat16)],
        compiler_params=params(LIMIT),
        name="queries",
    )(meta, near, far, *weights, cos, sin)


def attend_kernel(meta, dest, lengths, q_ref, c_mine, c_other, kv0, kv1, kv2, kv3, out):
    x = meta[2]
    g = meta[3]
    out[...] = jnp.zeros_like(out)
    row = lax.broadcasted_iota(jnp.int32, (256, 256), 0) & 63
    col = lax.broadcasted_iota(jnp.int32, (1, 256), 1)
    row_pos = (row >> 4) * 64 + x * 16 + (row & 15)
    which = col >> 6
    turn = jnp.where(which == 0, 0, jnp.where(which == 1, 3, jnp.where(which == 2, 1, 2)))
    col_pos = ((col & 63) >> 4) * 64 + ((x + turn) & 3) * 16 + (col & 15)
    causal = col_pos <= row_pos
    keys = jnp.concatenate([c_mine[:, :HD], c_other[:, :HD]], axis=0)
    values = jnp.concatenate([c_mine[:, HD:], c_other[:, HD:]], axis=0)
    contract = (((1,), (1,)), ((), ()))
    for i in range(RESP):
        length = lengths[g * RESP + i]
        q = q_ref[i].reshape(256, HD)
        self_keys = jnp.concatenate([ref[i, :, :HD] for ref in (kv0, kv1, kv2, kv3)], axis=0)
        self_values = jnp.concatenate([ref[i, :, HD:] for ref in (kv0, kv1, kv2, kv3)], axis=0)
        far = lax.dot_general(q, keys, contract, preferred_element_type=jnp.float32)
        near = lax.dot_general(q, self_keys, contract, preferred_element_type=jnp.float32)
        near = jnp.where(causal & (col_pos < length), near, -jnp.inf)
        top = jnp.maximum(
            jnp.max(far, axis=-1, keepdims=True), jnp.max(near, axis=-1, keepdims=True)
        ) * (SCALE * LOG2E)
        far = jnp.exp2(far * (SCALE * LOG2E) - top)
        near = jnp.exp2(near * (SCALE * LOG2E) - top)
        total = jnp.sum(far, axis=-1, keepdims=True) + jnp.sum(near, axis=-1, keepdims=True)
        mixed = jnp.dot(far.astype(jnp.bfloat16), values, preferred_element_type=jnp.float32)
        mixed = mixed + jnp.dot(
            near.astype(jnp.bfloat16), self_values, preferred_element_type=jnp.float32
        )
        mixed = jnp.where(row_pos[:, 0:HD] < length, mixed / total, 0.0).astype(jnp.bfloat16)
        out[dest[g * RESP + i]] = mixed.reshape(4, 64, HD)


def attend(meta, dest, lengths, q, c_mine, c_other, parts):
    return pl.pallas_call(
        attend_kernel,
        out_shape=jax.ShapeDtypeStruct((GROUPS, 4, 64, HD), jnp.bfloat16),
        in_specs=[SMEM_SPEC] * 3 + [VMEM_SPEC] * 7,
        out_specs=VMEM_SPEC,
        compiler_params=params(LIMIT),
        name="attend",
    )(meta, dest, lengths, q, c_mine, c_other, *parts)


def on_device(
    tokens, gain, w_query, b_query, w_key, b_key, w_value, b_value, rubric_cache, dest_of, lengths
):
    g = lax.axis_index("score")
    m = lax.axis_index("mp")
    z, c = g // 2, g % 2
    y, x = m // 4, m % 4
    meta = jnp.stack([y, c, x, g]).astype(jnp.int32)

    own = tokens.reshape(CHUNK, D)
    gain = gain.reshape(1, D)
    before = shift(own, dy=1)
    after = shift(own, dy=-1)
    far_a = shift(before[: CHUNK // 2], dy=1)
    far_b = shift(after[CHUNK // 2 :], dy=-1)

    frequency = jnp.exp(jnp.arange(64, dtype=jnp.float32) * (-2.0 * math.log(THETA) / HD))
    slot = jnp.arange(64, dtype=jnp.int32)
    positions = PROMPT + (slot // 16) * 64 + x * 16 + slot % 16
    angles = positions.astype(jnp.float32)[:, None] * frequency[None, :]
    cos = jnp.cos(angles)
    sin = jnp.sin(angles)
    cos = jnp.concatenate([cos, cos], axis=1)
    sin = jnp.concatenate([-sin, sin], axis=1)

    wk = lax.dynamic_slice_in_dim(w_key, y * HD, HD, 1)
    wv = lax.dynamic_slice_in_dim(w_value, y * HD, HD, 1)
    small = (gain, wk, wv, b_key.reshape(1, -1), b_value.reshape(1, -1), cos, sin)

    first = lax.reduce_precision(b_query, 8, 7)
    second = lax.reduce_precision(b_query - first, 8, 7)
    third = b_query - first - second
    tail = jnp.stack([first, second, third]).astype(jnp.bfloat16)
    tail = jnp.pad(tail, ((0, BIAS_ROWS - 3), (0, 0)))
    w_own = jnp.concatenate([w_query, tail], axis=0)
    w_beside = both_ways(w_own, "x")
    w_across = shift(w_beside, flip=1)
    w_far = both_ways(w_beside, "x")

    owner = dest_of[0]
    cache = rubric_cache[0]
    swapped = shift(cache, flip=1)
    cache = jnp.where(owner % 2 == c, cache, swapped)
    piece = lax.dynamic_slice_in_dim(cache, c * 64, 64, 1)
    beside = both_ways(cache, "z")
    z_far = shift(piece, dz=2)
    for_other = lax.dynamic_slice_in_dim(beside, (1 - c) * 64, 64, 1)
    beside = lax.dynamic_slice_in_dim(beside, c * 64, 64, 1)
    from_other = shift(for_other, flip=1)
    turn = (owner // 2 - z) % 4
    here = jnp.where(c == 0, 3, 1)
    piece = jnp.where(
        turn == 0, piece, jnp.where(turn == 2, z_far, jnp.where(turn == here, beside, from_other))
    )
    spread = jnp.broadcast_to(piece[:, None], (4, 4, 64, 2 * HD)).reshape(16, 64, 2 * HD)
    c_mine = lax.all_to_all(spread, "mp", 0, 0, tiled=True).reshape(1024, 2 * HD)

    kv, near_rows = keys_values(
        near_kernel, "near_rows", 3 * CHUNK, meta, (own, before, after), small
    )
    kv, far_rows = keys_values(far_kernel, "far_rows", CHUNK, meta, (kv, far_a, far_b), small)
    c_mine, _ = lax.optimization_barrier((c_mine, kv))
    c_other = shift(c_mine, flip=1)
    parts = (kv, shift(kv, dx=1), shift(kv, dx=-1), shift(kv, dx=2))
    far_rows, _ = lax.optimization_barrier((far_rows, c_other))
    weights = (w_own, w_beside, w_across, w_far)
    q = make_queries(meta, near_rows, far_rows, weights, cos, sin)
    ready = attend(meta, dest_of, lengths, q, c_mine, c_other, parts)
    arrived = lax.all_to_all(
        ready.reshape(32, 64, HD), AXES, 0, 0, tiled=True, axis_index_groups=SCORE_X_GROUPS
    )
    result = arrived.reshape(GROUPS, 4, 4, 16, HD).transpose(0, 2, 1, 3, 4)
    return result.reshape(1, GROUPS, LEN_MAX, HD)


def solution(mesh):
    in_specs = (
        P("score", "mp", None),
        P(),
        P(None, "mp"),
        P("mp"),
        P(),
        P(),
        P(),
        P(),
        P("score", None, "mp", None),
        P(),
        P(),
    )
    out_specs = P("score", None, None, "mp")
    return jax.shard_map(
        on_device, mesh=mesh, in_specs=in_specs, out_specs=out_specs, check_vma=False
    )
```

```python
import math

import jax
import jax.numpy as jnp
from jax import lax
from jax.experimental import pallas as pl
from jax.experimental.pallas import tpu as pltpu
from jax.sharding import PartitionSpec as P

D = 3584
KV_HEADS = 4
HD = 128
LEN_MAX = 256
PROMPT = 2048
RESP = 6
GROUPS = 8
BIAS_ROWS = 16
CHUNK = RESP * 16
THETA = 1000000.0
EPSILON = 1e-06
SCALE = 1.0 / math.sqrt(HD)
LIMIT = 36
LOG2E = math.log2(math.e)
AXES = ("score", "mp")


def device_number(x, y, z, c):
    return (z * 2 + c) * 16 + y * 4 + x


def shift(v, dx=0, dy=0, dz=0, flip=0):
    pairs = []
    for x in range(4):
        for y in range(4):
            for z in range(4):
                for c in range(2):
                    target = device_number((x + dx) % 4, (y + dy) % 4, (z + dz) % 4, c ^ flip)
                    pairs.append((device_number(x, y, z, c), target))
    return lax.ppermute(v, AXES, pairs)


def both_ways(v, axis, step=1):
    pairs = []
    for x in range(4):
        for y in range(4):
            for z in range(4):
                for c in range(2):
                    at = {"x": x, "y": y, "z": z}
                    at[axis] = (at[axis] + step * (1 - 2 * c)) % 4
                    pairs.append((device_number(x, y, z, c), device_number(**at, c=c)))
    return lax.ppermute(v, AXES, pairs)


SCORE_X_GROUPS = [[s * 16 + y * 4 + x for s in range(8) for x in range(4)] for y in range(4)]


def params(mib):
    return pltpu.CompilerParams(vmem_limit_bytes=mib * 1024 * 1024)


VMEM_SPEC = pl.BlockSpec(memory_space=pltpu.VMEM)
SMEM_SPEC = pl.BlockSpec(memory_space=pltpu.SMEM)


def rope(v, cos, sin):
    return v * cos + pltpu.roll(v, 64, axis=1) * sin


TURNS = (0, 3, 1, 2)


def chunk_y(y, j):
    return lax.rem(y + TURNS[j], 4)


def norm(tokens, gain):
    wide = tokens.astype(jnp.float32)
    mean = jnp.mean(wide * wide, axis=-1, keepdims=True)
    return (wide * lax.rsqrt(mean + EPSILON) * gain).astype(jnp.bfloat16)


def table(ref, y):
    base = pl.multiple_of(y * 16, 16)
    return base, ref[pl.ds(base, 16), :]


def project(y, rows, chunk_ids, wk, wv, bk, bv, cos_ref, sin_ref, out):
    w = jnp.concatenate([wk[...], wv[...]], axis=1)
    both = jnp.dot(rows, w, preferred_element_type=jnp.float32)
    at = pl.multiple_of(y * HD, HD)
    key = both[:, :HD] + bk[:, pl.ds(at, HD)]
    value = (both[:, HD:] + bv[:, pl.ds(at, HD)]).astype(jnp.bfloat16)
    for n, j in enumerate(chunk_ids):
        base, cos = table(cos_ref, chunk_y(y, j))
        ignored, sin = table(sin_ref, chunk_y(y, j))
        for i in range(RESP):
            part = slice(n * CHUNK + i * 16, n * CHUNK + i * 16 + 16)
            out[i, pl.ds(base, 16), 0:HD] = rope(key[part], cos, sin).astype(jnp.bfloat16)
            out[i, pl.ds(base, 16), HD : 2 * HD] = value[part]


def near_kernel(meta, own, before, after, gain, wk, wv, bk, bv, cos_ref, sin_ref, out, rows):
    out[...] = jnp.zeros_like(out)
    rows[0:CHUNK, :] = norm(own[...], gain[...])
    rows[CHUNK : 2 * CHUNK, :] = norm(before[...], gain[...])
    rows[2 * CHUNK : 3 * CHUNK, :] = norm(after[...], gain[...])
    project(meta[0], rows[...], (0, 1, 2), wk, wv, bk, bv, cos_ref, sin_ref, out)


def far_kernel(meta, near, far_a, far_b, gain, wk, wv, bk, bv, cos_ref, sin_ref, out, rows):
    out[...] = near[...]
    rows[0 : CHUNK // 2, :] = norm(far_a[...], gain[...])
    rows[CHUNK // 2 : CHUNK, :] = norm(far_b[...], gain[...])
    project(meta[0], rows[...], (3,), wk, wv, bk, bv, cos_ref, sin_ref, out)


def keys_values(kernel, name, count, meta, chunks, small):
    return pl.pallas_call(
        kernel,
        out_shape=(
            jax.ShapeDtypeStruct((RESP, 64, 2 * HD), jnp.bfloat16),
            jax.ShapeDtypeStruct((count, D), jnp.bfloat16),
        ),
        in_specs=[SMEM_SPEC] + [VMEM_SPEC] * (len(chunks) + len(small)),
        out_specs=(VMEM_SPEC, VMEM_SPEC),
        compiler_params=params(LIMIT),
        name=name,
    )(meta, *chunks, *small)


def query_kernel(meta, near, far, w0, w1, w2, w3, cos_ref, sin_ref, q_out, rows):
    y, c, x = meta[0], meta[1], meta[2]
    rows[0 : 3 * CHUNK, :] = near[...]
    rows[3 * CHUNK : 4 * CHUNK, :] = far[...]
    weights = (w0, w1, w2, w3)
    heads = [lax.rem(x + turn, 4) for turn in (0, 3 - 2 * c, 1 + 2 * c, 2)]
    for lo in (0, 2):
        w = jnp.concatenate([weights[lo][:D, :], weights[lo + 1][:D, :]], axis=1)
        both = jnp.dot(rows[...], w, preferred_element_type=jnp.float32)
        for n in (lo, lo + 1):
            tail = weights[n][D : D + BIAS_ROWS, :].astype(jnp.float32)
            bias = tail[0:1, :] + tail[1:2, :] + tail[2:3, :]
            raw = both[:, (n - lo) * HD : (n - lo + 1) * HD] + bias
            for j in range(4):
                base, cos = table(cos_ref, chunk_y(y, j))
                ignored, sin = table(sin_ref, chunk_y(y, j))
                for i in range(RESP):
                    part = raw[j * CHUNK + i * 16 : j * CHUNK + i * 16 + 16, :]
                    rotated = rope(part, cos, sin).astype(jnp.bfloat16)
                    q_out[i, heads[n], pl.ds(base, 16), :] = rotated


def make_queries(meta, near, far, weights, cos, sin):
    return pl.pallas_call(
        query_kernel,
        out_shape=jax.ShapeDtypeStruct((RESP, 4, 64, HD), jnp.bfloat16),
        in_specs=[SMEM_SPEC] + [VMEM_SPEC] * 8,
        out_specs=VMEM_SPEC,
        scratch_shapes=[pltpu.VMEM((4 * CHUNK, D), jnp.bfloat16)],
        compiler_params=params(LIMIT),
        name="queries",
    )(meta, near, far, *weights, cos, sin)


def attend_kernel(meta, dest, lengths, q_ref, c_mine, c_other, kv0, kv1, kv2, kv3, out):
    x = meta[2]
    g = meta[3]
    out[...] = jnp.zeros_like(out)
    row = lax.broadcasted_iota(jnp.int32, (256, 256), 0) & 63
    col = lax.broadcasted_iota(jnp.int32, (1, 256), 1)
    row_pos = (row >> 4) * 64 + x * 16 + (row & 15)
    which = col >> 6
    turn = jnp.where(which == 0, 0, jnp.where(which == 1, 3, jnp.where(which == 2, 1, 2)))
    col_pos = ((col & 63) >> 4) * 64 + ((x + turn) & 3) * 16 + (col & 15)
    causal = col_pos <= row_pos
    keys = jnp.concatenate([c_mine[:, :HD], c_other[:, :HD]], axis=0)
    values = jnp.concatenate([c_mine[:, HD:], c_other[:, HD:]], axis=0)
    contract = (((1,), (1,)), ((), ()))
    for i in range(RESP):
        length = lengths[g * RESP + i]
        q = q_ref[i].reshape(256, HD)
        self_keys = jnp.concatenate([ref[i, :, :HD] for ref in (kv0, kv1, kv2, kv3)], axis=0)
        self_values = jnp.concatenate([ref[i, :, HD:] for ref in (kv0, kv1, kv2, kv3)], axis=0)
        far = lax.dot_general(q, keys, contract, preferred_element_type=jnp.float32)
        near = lax.dot_general(q, self_keys, contract, preferred_element_type=jnp.float32)
        near = jnp.where(causal & (col_pos < length), near, -jnp.inf)
        top = jnp.maximum(
            jnp.max(far, axis=-1, keepdims=True), jnp.max(near, axis=-1, keepdims=True)
        ) * (SCALE * LOG2E)
        far = jnp.exp2(far * (SCALE * LOG2E) - top)
        near = jnp.exp2(near * (SCALE * LOG2E) - top)
        total = jnp.sum(far, axis=-1, keepdims=True) + jnp.sum(near, axis=-1, keepdims=True)
        mixed = jnp.dot(far.astype(jnp.bfloat16), values, preferred_element_type=jnp.float32)
        mixed = mixed + jnp.dot(
            near.astype(jnp.bfloat16), self_values, preferred_element_type=jnp.float32
        )
        mixed = mixed * (1.0 / total)
        mixed = jnp.where(row_pos[:, 0:HD] < length, mixed, 0.0).astype(jnp.bfloat16)
        out[dest[g * RESP + i]] = mixed.reshape(4, 64, HD)


def attend(meta, dest, lengths, q, c_mine, c_other, parts):
    return pl.pallas_call(
        attend_kernel,
        out_shape=jax.ShapeDtypeStruct((GROUPS, 4, 64, HD), jnp.bfloat16),
        in_specs=[SMEM_SPEC] * 3 + [VMEM_SPEC] * 7,
        out_specs=VMEM_SPEC,
        compiler_params=params(LIMIT),
        name="attend",
    )(meta, dest, lengths, q, c_mine, c_other, *parts)


def on_device(
    tokens, gain, w_query, b_query, w_key, b_key, w_value, b_value, rubric_cache, dest_of, lengths
):
    g = lax.axis_index("score")
    m = lax.axis_index("mp")
    z, c = g // 2, g % 2
    y, x = m // 4, m % 4
    meta = jnp.stack([y, c, x, g]).astype(jnp.int32)

    own = tokens.reshape(CHUNK, D)
    gain = gain.reshape(1, D)
    before = shift(own, dy=1)
    after = shift(own, dy=-1)
    far_a = shift(before[: CHUNK // 2], dy=1)
    far_b = shift(after[CHUNK // 2 :], dy=-1)

    frequency = jnp.exp(jnp.arange(64, dtype=jnp.float32) * (-2.0 * math.log(THETA) / HD))
    slot = jnp.arange(64, dtype=jnp.int32)
    positions = PROMPT + (slot // 16) * 64 + x * 16 + slot % 16
    angles = positions.astype(jnp.float32)[:, None] * frequency[None, :]
    cos = jnp.cos(angles)
    sin = jnp.sin(angles)
    cos = jnp.concatenate([cos, cos], axis=1)
    sin = jnp.concatenate([-sin, sin], axis=1)

    wk = lax.dynamic_slice_in_dim(w_key, y * HD, HD, 1)
    wv = lax.dynamic_slice_in_dim(w_value, y * HD, HD, 1)
    small = (gain, wk, wv, b_key.reshape(1, -1), b_value.reshape(1, -1), cos, sin)

    first = lax.reduce_precision(b_query, 8, 7)
    second = lax.reduce_precision(b_query - first, 8, 7)
    third = b_query - first - second
    tail = jnp.stack([first, second, third]).astype(jnp.bfloat16)
    tail = jnp.pad(tail, ((0, BIAS_ROWS - 3), (0, 0)))
    w_own = jnp.concatenate([w_query, tail], axis=0)
    w_beside = both_ways(w_own, "x")
    w_across = shift(w_beside, flip=1)
    w_far = both_ways(w_beside, "x")

    owner = dest_of[0]
    cache = rubric_cache[0]
    swapped = shift(cache, flip=1)
    cache = jnp.where(owner % 2 == c, cache, swapped)
    piece = lax.dynamic_slice_in_dim(cache, c * 64, 64, 1)
    beside = both_ways(cache, "z")
    z_far = shift(piece, dz=2)
    for_other = lax.dynamic_slice_in_dim(beside, (1 - c) * 64, 64, 1)
    beside = lax.dynamic_slice_in_dim(beside, c * 64, 64, 1)
    from_other = shift(for_other, flip=1)
    turn = (owner // 2 - z) % 4
    here = jnp.where(c == 0, 3, 1)
    piece = jnp.where(
        turn == 0, piece, jnp.where(turn == 2, z_far, jnp.where(turn == here, beside, from_other))
    )
    spread = jnp.broadcast_to(piece[:, None], (4, 4, 64, 2 * HD)).reshape(16, 64, 2 * HD)
    c_mine = lax.all_to_all(spread, "mp", 0, 0, tiled=True).reshape(1024, 2 * HD)

    kv, near_rows = keys_values(
        near_kernel, "near_rows", 3 * CHUNK, meta, (own, before, after), small
    )
    kv, far_rows = keys_values(far_kernel, "far_rows", CHUNK, meta, (kv, far_a, far_b), small)
    c_mine, _ = lax.optimization_barrier((c_mine, kv))
    c_other = shift(c_mine, flip=1)
    two_away = shift(kv, dx=2)
    parts = (kv, shift(kv, dx=1), shift(kv, dx=-1), two_away)
    far_rows, _ = lax.optimization_barrier((far_rows, c_other))
    weights = (w_own, w_beside, w_across, w_far)
    q = make_queries(meta, near_rows, far_rows, weights, cos, sin)
    ready = attend(meta, dest_of, lengths, q, c_mine, c_other, parts)
    arrived = lax.all_to_all(
        ready.reshape(32, 64, HD), AXES, 0, 0, tiled=True, axis_index_groups=SCORE_X_GROUPS
    )
    result = arrived.reshape(GROUPS, 4, 4, 16, HD).transpose(0, 2, 1, 3, 4)
    return result.reshape(1, GROUPS, LEN_MAX, HD)


def solution(mesh):
    in_specs = (
        P("score", "mp", None),
        P(),
        P(None, "mp"),
        P("mp"),
        P(),
        P(),
        P(),
        P(),
        P("score", None, "mp", None),
        P(),
        P(),
    )
    out_specs = P("score", None, None, "mp")
    return jax.shard_map(
        on_device, mesh=mesh, in_specs=in_specs, out_specs=out_specs, check_vma=False
    )
```

```python
import math

import jax
import jax.numpy as jnp
from jax import lax
from jax.experimental import pallas as pl
from jax.experimental.pallas import tpu as pltpu
from jax.sharding import PartitionSpec as P

D = 3584
KV_HEADS = 4
HD = 128
LEN_MAX = 256
PROMPT = 2048
RESP = 6
GROUPS = 8
BIAS_ROWS = 16
CHUNK = RESP * 16
THETA = 1000000.0
EPSILON = 1e-06
SCALE = 1.0 / math.sqrt(HD)
LIMIT = 36
LOG2E = math.log2(math.e)
AXES = ("score", "mp")


def device_number(x, y, z, c):
    return (z * 2 + c) * 16 + y * 4 + x


def shift(v, dx=0, dy=0, dz=0, flip=0):
    pairs = []
    for x in range(4):
        for y in range(4):
            for z in range(4):
                for c in range(2):
                    target = device_number((x + dx) % 4, (y + dy) % 4, (z + dz) % 4, c ^ flip)
                    pairs.append((device_number(x, y, z, c), target))
    return lax.ppermute(v, AXES, pairs)


def both_ways(v, axis, step=1):
    pairs = []
    for x in range(4):
        for y in range(4):
            for z in range(4):
                for c in range(2):
                    at = {"x": x, "y": y, "z": z}
                    at[axis] = (at[axis] + step * (1 - 2 * c)) % 4
                    pairs.append((device_number(x, y, z, c), device_number(**at, c=c)))
    return lax.ppermute(v, AXES, pairs)


SCORE_X_GROUPS = [[s * 16 + y * 4 + x for s in range(8) for x in range(4)] for y in range(4)]


def params(mib):
    return pltpu.CompilerParams(vmem_limit_bytes=mib * 1024 * 1024)


VMEM_SPEC = pl.BlockSpec(memory_space=pltpu.VMEM)
ANY_SPEC = pl.BlockSpec(memory_space=pl.ANY)
SMEM_SPEC = pl.BlockSpec(memory_space=pltpu.SMEM)


def rope(v, cos, sin):
    return v * cos + pltpu.roll(v, 64, axis=1) * sin


TURNS = (0, 3, 1, 2)


def chunk_y(y, j):
    return lax.rem(y + TURNS[j], 4)


def norm(tokens, gain):
    wide = tokens.astype(jnp.float32)
    mean = jnp.mean(wide * wide, axis=-1, keepdims=True)
    return (wide * lax.rsqrt(mean + EPSILON) * gain).astype(jnp.bfloat16)


def table(ref, y):
    base = pl.multiple_of(y * 16, 16)
    return base, ref[pl.ds(base, 16), :]


def project(y, rows, chunk_ids, wk, wv, bk, bv, cos_ref, sin_ref, out):
    w = jnp.concatenate([wk[...], wv[...]], axis=1)
    both = jnp.dot(rows, w, preferred_element_type=jnp.float32)
    at = pl.multiple_of(y * HD, HD)
    key = both[:, :HD] + bk[:, pl.ds(at, HD)]
    value = (both[:, HD:] + bv[:, pl.ds(at, HD)]).astype(jnp.bfloat16)
    for n, j in enumerate(chunk_ids):
        base, cos = table(cos_ref, chunk_y(y, j))
        ignored, sin = table(sin_ref, chunk_y(y, j))
        for i in range(RESP):
            part = slice(n * CHUNK + i * 16, n * CHUNK + i * 16 + 16)
            out[i, pl.ds(base, 16), 0:HD] = rope(key[part], cos, sin).astype(jnp.bfloat16)
            out[i, pl.ds(base, 16), HD : 2 * HD] = value[part]


def near_kernel(meta, own, before, after, gain, wk, wv, bk, bv, cos_ref, sin_ref, out, rows):
    out[...] = jnp.zeros_like(out)
    rows[0:CHUNK, :] = norm(own[...], gain[...])
    rows[CHUNK : 2 * CHUNK, :] = norm(before[...], gain[...])
    rows[2 * CHUNK : 3 * CHUNK, :] = norm(after[...], gain[...])
    project(meta[0], rows[...], (0, 1, 2), wk, wv, bk, bv, cos_ref, sin_ref, out)


def far_kernel(meta, near, far_a, far_b, gain, wk, wv, bk, bv, cos_ref, sin_ref, out, rows):
    out[...] = near[...]
    rows[0 : CHUNK // 2, :] = norm(far_a[...], gain[...])
    rows[CHUNK // 2 : CHUNK, :] = norm(far_b[...], gain[...])
    project(meta[0], rows[...], (3,), wk, wv, bk, bv, cos_ref, sin_ref, out)


def keys_values(kernel, name, count, meta, chunks, small):
    return pl.pallas_call(
        kernel,
        out_shape=(
            jax.ShapeDtypeStruct((RESP, 64, 2 * HD), jnp.bfloat16),
            jax.ShapeDtypeStruct((count, D), jnp.bfloat16),
        ),
        in_specs=[SMEM_SPEC] + [VMEM_SPEC] * (len(chunks) + len(small)),
        out_specs=(VMEM_SPEC, VMEM_SPEC),
        compiler_params=params(LIMIT),
        name=name,
    )(meta, *chunks, *small)


def query_kernel(
    meta, near, far, w0, w1, w2, w3, cos_ref, sin_ref, q_out, rows, buf, sems
):
    y, c, x = meta[0], meta[1], meta[2]
    copies = [
        pltpu.make_async_copy(ref, buf.at[n], sems.at[n]) for n, ref in enumerate((w0, w1, w2, w3))
    ]
    for copy in copies:
        copy.start()
    rows[0 : 3 * CHUNK, :] = near[...]
    rows[3 * CHUNK : 4 * CHUNK, :] = far[...]
    heads = [lax.rem(x + turn, 4) for turn in (0, 3 - 2 * c, 1 + 2 * c, 2)]
    for lo in (0, 2):
        copies[lo].wait()
        copies[lo + 1].wait()
        w = jnp.concatenate([buf[lo, :D, :], buf[lo + 1, :D, :]], axis=1)
        both = jnp.dot(rows[...], w, preferred_element_type=jnp.float32)
        for n in (lo, lo + 1):
            tail = buf[n, D : D + BIAS_ROWS, :].astype(jnp.float32)
            bias = tail[0:1, :] + tail[1:2, :] + tail[2:3, :]
            raw = both[:, (n - lo) * HD : (n - lo + 1) * HD] + bias
            for j in range(4):
                base, cos = table(cos_ref, chunk_y(y, j))
                ignored, sin = table(sin_ref, chunk_y(y, j))
                for i in range(RESP):
                    part = raw[j * CHUNK + i * 16 : j * CHUNK + i * 16 + 16, :]
                    rotated = rope(part, cos, sin).astype(jnp.bfloat16)
                    q_out[i, heads[n], pl.ds(base, 16), :] = rotated


def make_queries(meta, near, far, weights, cos, sin):
    return pl.pallas_call(
        query_kernel,
        out_shape=jax.ShapeDtypeStruct((RESP, 4, 64, HD), jnp.bfloat16),
        in_specs=[SMEM_SPEC] + [VMEM_SPEC] * 2 + [ANY_SPEC] * 4 + [VMEM_SPEC] * 2,
        out_specs=VMEM_SPEC,
        scratch_shapes=[
            pltpu.VMEM((4 * CHUNK, D), jnp.bfloat16),
            pltpu.VMEM((4, D + BIAS_ROWS, HD), jnp.bfloat16),
            pltpu.SemaphoreType.DMA((4,)),
        ],
        compiler_params=params(50),
        name="queries",
    )(meta, near, far, *weights, cos, sin)


def attend_kernel(meta, dest, lengths, q_ref, c_mine, c_other, kv0, kv1, kv2, kv3, out):
    x = meta[2]
    g = meta[3]
    out[...] = jnp.zeros_like(out)
    row = lax.broadcasted_iota(jnp.int32, (256, 256), 0) & 63
    col = lax.broadcasted_iota(jnp.int32, (1, 256), 1)
    row_pos = (row >> 4) * 64 + x * 16 + (row & 15)
    which = col >> 6
    turn = jnp.where(which == 0, 0, jnp.where(which == 1, 3, jnp.where(which == 2, 1, 2)))
    col_pos = ((col & 63) >> 4) * 64 + ((x + turn) & 3) * 16 + (col & 15)
    causal = col_pos <= row_pos
    keys = jnp.concatenate([c_mine[:, :HD], c_other[:, :HD]], axis=0)
    values = jnp.concatenate([c_mine[:, HD:], c_other[:, HD:]], axis=0)
    contract = (((1,), (1,)), ((), ()))
    for i in range(RESP):
        length = lengths[g * RESP + i]
        q = q_ref[i].reshape(256, HD)
        self_keys = jnp.concatenate([ref[i, :, :HD] for ref in (kv0, kv1, kv2, kv3)], axis=0)
        self_values = jnp.concatenate([ref[i, :, HD:] for ref in (kv0, kv1, kv2, kv3)], axis=0)
        far = lax.dot_general(q, keys, contract, preferred_element_type=jnp.float32)
        near = lax.dot_general(q, self_keys, contract, preferred_element_type=jnp.float32)
        near = jnp.where(causal & (col_pos < length), near, -jnp.inf)
        top = jnp.maximum(
            jnp.max(far, axis=-1, keepdims=True), jnp.max(near, axis=-1, keepdims=True)
        ) * (SCALE * LOG2E)
        far = jnp.exp2(far * (SCALE * LOG2E) - top)
        near = jnp.exp2(near * (SCALE * LOG2E) - top)
        total = jnp.sum(far, axis=-1, keepdims=True) + jnp.sum(near, axis=-1, keepdims=True)
        mixed = jnp.dot(far.astype(jnp.bfloat16), values, preferred_element_type=jnp.float32)
        mixed = mixed + jnp.dot(
            near.astype(jnp.bfloat16), self_values, preferred_element_type=jnp.float32
        )
        mixed = jnp.where(row_pos[:, 0:HD] < length, mixed / total, 0.0).astype(jnp.bfloat16)
        out[dest[g * RESP + i]] = mixed.reshape(4, 64, HD)


def attend(meta, dest, lengths, q, c_mine, c_other, parts):
    return pl.pallas_call(
        attend_kernel,
        out_shape=jax.ShapeDtypeStruct((GROUPS, 4, 64, HD), jnp.bfloat16),
        in_specs=[SMEM_SPEC] * 3 + [VMEM_SPEC] * 7,
        out_specs=VMEM_SPEC,
        compiler_params=params(LIMIT),
        name="attend",
    )(meta, dest, lengths, q, c_mine, c_other, *parts)


def on_device(
    tokens, gain, w_query, b_query, w_key, b_key, w_value, b_value, rubric_cache, dest_of, lengths
):
    g = lax.axis_index("score")
    m = lax.axis_index("mp")
    z, c = g // 2, g % 2
    y, x = m // 4, m % 4
    meta = jnp.stack([y, c, x, g]).astype(jnp.int32)

    own = tokens.reshape(CHUNK, D)
    gain = gain.reshape(1, D)
    before = shift(own, dy=1)
    after = shift(own, dy=-1)
    far_a = shift(before[: CHUNK // 2], dy=1)
    far_b = shift(after[CHUNK // 2 :], dy=-1)

    frequency = jnp.exp(jnp.arange(64, dtype=jnp.float32) * (-2.0 * math.log(THETA) / HD))
    slot = jnp.arange(64, dtype=jnp.int32)
    positions = PROMPT + (slot // 16) * 64 + x * 16 + slot % 16
    angles = positions.astype(jnp.float32)[:, None] * frequency[None, :]
    cos = jnp.cos(angles)
    sin = jnp.sin(angles)
    cos = jnp.concatenate([cos, cos], axis=1)
    sin = jnp.concatenate([-sin, sin], axis=1)

    wk = lax.dynamic_slice_in_dim(w_key, y * HD, HD, 1)
    wv = lax.dynamic_slice_in_dim(w_value, y * HD, HD, 1)
    small = (gain, wk, wv, b_key.reshape(1, -1), b_value.reshape(1, -1), cos, sin)

    first = lax.reduce_precision(b_query, 8, 7)
    second = lax.reduce_precision(b_query - first, 8, 7)
    third = b_query - first - second
    tail = jnp.stack([first, second, third]).astype(jnp.bfloat16)
    tail = jnp.pad(tail, ((0, BIAS_ROWS - 3), (0, 0)))
    w_own = jnp.concatenate([w_query, tail], axis=0)
    w_beside = both_ways(w_own, "x")
    w_across = shift(w_beside, flip=1)
    w_far = both_ways(w_beside, "x")

    owner = dest_of[0]
    cache = rubric_cache[0]
    swapped = shift(cache, flip=1)
    cache = jnp.where(owner % 2 == c, cache, swapped)
    piece = lax.dynamic_slice_in_dim(cache, c * 64, 64, 1)
    beside = both_ways(cache, "z")
    z_far = shift(piece, dz=2)
    for_other = lax.dynamic_slice_in_dim(beside, (1 - c) * 64, 64, 1)
    beside = lax.dynamic_slice_in_dim(beside, c * 64, 64, 1)
    from_other = shift(for_other, flip=1)
    turn = (owner // 2 - z) % 4
    here = jnp.where(c == 0, 3, 1)
    piece = jnp.where(
        turn == 0, piece, jnp.where(turn == 2, z_far, jnp.where(turn == here, beside, from_other))
    )
    spread = jnp.broadcast_to(piece[:, None], (4, 4, 64, 2 * HD)).reshape(16, 64, 2 * HD)
    c_mine = lax.all_to_all(spread, "mp", 0, 0, tiled=True).reshape(1024, 2 * HD)

    kv, near_rows = keys_values(
        near_kernel, "near_rows", 3 * CHUNK, meta, (own, before, after), small
    )
    kv, far_rows = keys_values(far_kernel, "far_rows", CHUNK, meta, (kv, far_a, far_b), small)
    c_mine, _ = lax.optimization_barrier((c_mine, kv))
    c_other = shift(c_mine, flip=1)
    parts = (kv, shift(kv, dx=1), shift(kv, dx=-1), shift(kv, dx=2))
    far_rows, _ = lax.optimization_barrier((far_rows, c_other))
    weights = (w_own, w_beside, w_across, w_far)
    q = make_queries(meta, near_rows, far_rows, weights, cos, sin)
    ready = attend(meta, dest_of, lengths, q, c_mine, c_other, parts)
    arrived = lax.all_to_all(
        ready.reshape(32, 64, HD), AXES, 0, 0, tiled=True, axis_index_groups=SCORE_X_GROUPS
    )
    result = arrived.reshape(GROUPS, 4, 4, 16, HD).transpose(0, 2, 1, 3, 4)
    return result.reshape(1, GROUPS, LEN_MAX, HD)


def solution(mesh):
    in_specs = (
        P("score", "mp", None),
        P(),
        P(None, "mp"),
        P("mp"),
        P(),
        P(),
        P(),
        P(),
        P("score", None, "mp", None),
        P(),
        P(),
    )
    out_specs = P("score", None, None, "mp")
    return jax.shard_map(
        on_device, mesh=mesh, in_specs=in_specs, out_specs=out_specs, check_vma=False
    )
```
